32 devices in a mesh: groups: 2 (over y), tiles: 4 (over z), heads: 2 (over x), cfg: 2 (over core).
Axes of the slice: x: 2, y: 2, z: 4, core: 2. Of those that a mesh axis runs over, the one named last changes fastest.
Arguments:
- latents: bfloat16 [6144, 3072], P(('groups', 'tiles'), ('heads', 'cfg')), parts along dimension 0, may hold values from -6 to 6
- modulation: float32 [6, 3072], P('groups'), parts along dimension 0, may hold values from -3 to 3
- qkv_weight: bfloat16 [3072, 1536], P(None, ('heads', 'cfg')), may hold values from -0.109375 to 0.109375
- query_gain: float32 [128], replicated, may hold values from 0.25 to 1.75
- key_gain: float32 [128], replicated, may hold values from 0.25 to 1.75
- text_kv: bfloat16 [512, 1024], P('groups', ('heads', 'cfg')), parts along dimension 0, may hold values from -72 to 72
- text_len: int32 [2], P('groups'), parts along dimension 0, may hold values from 128 to 256
- tile_ids: int32 [16], P(('groups', 'tiles')), parts along dimension 0, may hold values from 0 to 7, as said below
- windows: int32 [16, 27], P('groups'), parts along dimension 0, may hold values from 0 to 7, as said below
- proj_weight: bfloat16 [512, 3072], P(None, ('heads', 'cfg')), may hold values from -0.25 to 0.25
Outputs:
- updated: bfloat16 [6144, 3072], P(('groups', 'tiles'), ('heads', 'cfg')), parts along dimension 0
The draws below stay inside these ranges and needn't reach their ends.
There are 2 independent parts, one for each index of `groups`. The reference program is written for one: setup_inputs(seed, part) draws one part's arguments, and reference() takes and returns one part's arrays. A program takes and returns all parts, laid end to end along the dimension named above; an argument that names none is the same for every part. Nothing has to cross between parts.
Inputs may be any that keep to these rules, and one draw needn't show every extreme that they name: Every entry of windows[t] names a tile at most one tile away from t along each dimension of the 2 x 2 x 2 tile grid, tile id (i * 2 + h) * 2 + w; entry 13 is t itself, and entries that name no other tile repeat t. `tile_ids`: slot s holds a tile id from (s // 2) * 2 to (s // 2) * 2 + 1; every id appears once.
All inputs are finite; a program needn't handle non-finite values.
Results may differ from the reference program's by a relative error of at most 0.0033.
The reference program's roundings to bfloat16 on the way (of `modulated`, `rounded` and `attended`) count: a program that leaves them out, or rounds other values in their place, can miss the bound.
Values may be sent and summed in bfloat16 or wider, within the bound.
No kernel may reach another device: no remote copies, remote signals or barrier semaphores. Data moves between devices by JAX's collectives and lax.ppermute only.
A program may use at most 64 MiB of HBM per device.

```python
import math
import jax
import jax.numpy as jnp
from jax import lax

D = 3072
HD = 128
TILE = 384
TPD = 2
TH = 2
TW = 2
TXT = 256
HEADS = 4
NTILES = 8
TT = 2
TOKENS = 3072


def draw_windows(key, part):
    key = jax.random.fold_in(key, 11)
    ident = jnp.arange(NTILES, dtype=jnp.int32)
    along_t = ident // (TH * TW)
    along_h = ident // TW % TH
    along_w = ident % TW
    radii = (jax.random.randint(key, (NTILES, 3), 0, 10) < 7).astype(jnp.int32)
    entries = []
    for shift_t in (-1, 0, 1):
        for shift_h in (-1, 0, 1):
            for shift_w in (-1, 0, 1):
                place_t = along_t + shift_t
                place_h = along_h + shift_h
                place_w = along_w + shift_w
                inside = (place_t >= 0) & (place_t < TT) & (place_h >= 0) & (place_h < TH) & (place_w >= 0) & (place_w < TW)
                reach = (abs(shift_t) <= radii[:, 0]) & (abs(shift_h) <= radii[:, 1]) & (abs(shift_w) <= radii[:, 2])
                other = (place_t * TH + place_h) * TW + place_w
                entries.append(jnp.where(inside & reach, other, ident))
    return jnp.stack(entries, axis=1).astype(jnp.int32)


def draw_tile_ids(key, part):
    key = jax.random.fold_in(key, 7)
    slabs = NTILES // TPD
    ranks = jax.random.randint(key, (slabs, TPD), 0, 1 << 20) * TPD + jnp.arange(TPD, dtype=jnp.int32)[None, :]
    order = jnp.argsort(ranks, axis=1).astype(jnp.int32)
    first = (jnp.arange(slabs, dtype=jnp.int32) * TPD)[:, None]
    return (first + order).reshape(NTILES).astype(jnp.int32)


def draw_text_kv(key, part):
    key = jax.random.fold_in(key, 5)
    first = jax.random.fold_in(key, 0)
    base = jax.random.normal(first, (TXT, HEADS, 2, HD), jnp.float32)
    return base.reshape(TXT, 2 * HEADS * HD).astype(jnp.bfloat16)


def levels(stream_key, shape, pieces, least, top_value):
    level, own = 1.0, jax.random.fold_in(stream_key, 6)
    for dim, parts in pieces:
        heights = jnp.exp(jax.random.uniform(jax.random.fold_in(own, dim), (parts,), jnp.float32, least / len(pieces), top_value / len(pieces)))
        level = level * jnp.repeat(heights, shape[dim] // parts).reshape([-1 if axis == dim else 1 for axis in range(len(shape))])
    return level


def scatter_about(rng, dims, deviation, bound, pieces=(), kind=jnp.bfloat16):
    level = levels(rng, dims, pieces, -0.22, 0.18) if pieces else 1.0
    drawn = jax.random.normal(rng, dims, jnp.float32) * deviation * level
    return jnp.minimum(jnp.maximum(drawn, -bound), bound).astype(kind)


def setup_inputs(seed: int = 0, part: int = 0) -> dict:
    arg_keys = jax.random.split(jax.random.key(seed), 11)
    own_keys = jax.random.split(jax.random.fold_in(arg_keys[10], part), 11)
    return {
        "latents": scatter_about(own_keys[0], (TOKENS, D), 1.0, 6.0, ((0, 4), (1, 4))),
        "modulation": scatter_about(own_keys[1], (3, D), 0.5, 3.0, (), jnp.float32),
        "qkv_weight": scatter_about(arg_keys[2], (D, 3 * HEADS * HD), D ** -0.5, 0.109375, ((1, 4),)),
        "query_gain": jnp.clip(1.0 + 0.15 * jax.random.normal(arg_keys[3], (HD,), jnp.float32), 0.25, 1.75),
        "key_gain": jnp.clip(1.0 + 0.15 * jax.random.normal(arg_keys[4], (HD,), jnp.float32), 0.25, 1.75),
        "text_kv": draw_text_kv(jax.random.fold_in(jax.random.fold_in(arg_keys[10], part), 71), part),
        "text_len": jax.random.randint(own_keys[6], (1,), TXT // 2, TXT + 1).astype(jnp.int32),
        "tile_ids": draw_tile_ids(jax.random.fold_in(jax.random.fold_in(arg_keys[10], part), 71), part),
        "windows": draw_windows(jax.random.fold_in(jax.random.fold_in(arg_keys[10], part), 71), part),
        "proj_weight": scatter_about(arg_keys[9], (HEADS * HD, D), (HEADS * HD) ** -0.5, 0.25, ((1, 4),)),
    }


epsilon = 1e-06

def rms_norm(values, gain):
    return values * lax.rsqrt(lax.optimization_barrier(jnp.mean(values * values, axis=-1, keepdims=True)) + epsilon) * gain

def round_trip(values):
    return lax.optimization_barrier(values.astype(jnp.bfloat16)).astype(jnp.float32)

def reference(latents, modulation, qkv_weight, query_gain, key_gain, text_kv, text_len, tile_ids, windows, proj_weight):
    rows = latents.astype(jnp.float32)
    average = lax.optimization_barrier(jnp.mean(rows, axis=-1, keepdims=True))
    centred = rows - average
    spread = lax.optimization_barrier(jnp.mean(centred * centred, axis=-1, keepdims=True))
    modulated = (centred * lax.rsqrt(spread + epsilon) * (1.0 + modulation[1]) + modulation[0]).astype(jnp.bfloat16)
    projected = jnp.dot(modulated, qkv_weight, preferred_element_type=jnp.float32).reshape(TOKENS, HEADS, 3, HD)
    queries = round_trip(rms_norm(projected[:, :, 0], query_gain))
    keys = round_trip(rms_norm(projected[:, :, 1], key_gain))
    values = round_trip(projected[:, :, 2])
    text_pair = text_kv.astype(jnp.float32).reshape(TXT, HEADS, 2, HD)
    all_keys = jnp.concatenate([keys, text_pair[:, :, 0]], axis=0)
    all_values = jnp.concatenate([values, text_pair[:, :, 1]], axis=0)
    slot_windows = windows[tile_ids]
    allowed = jnp.any(slot_windows[:, :, None] == tile_ids[None, None, :], axis=1)
    text_live = jnp.arange(TXT, dtype=jnp.int32) < text_len[0]
    factor = 1.0 / math.sqrt(HD)

    def one_tile(slot):
        start = (slot * TILE).astype(jnp.int32)
        rows_q = lax.dynamic_slice_in_dim(queries, start, TILE, 0)
        image_live = jnp.repeat(allowed[slot], TILE)
        live = jnp.concatenate([image_live, text_live])
        scores = jnp.einsum('qhd,khd->hqk', rows_q, all_keys, precision=lax.Precision.HIGHEST) * factor
        scores = jnp.where(live[None, None, :], scores, -jnp.inf)
        largest = lax.optimization_barrier(jnp.max(scores, axis=-1, keepdims=True))
        weights = jnp.exp(scores - largest)
        total = lax.optimization_barrier(jnp.sum(weights, axis=-1, keepdims=True))
        rounded = round_trip(weights)
        result = jnp.einsum('hqk,khd->qhd', rounded, all_values, precision=lax.Precision.HIGHEST)
        result = result / jnp.transpose(total, (1, 0, 2))
        return result.reshape(TILE, HEADS * HD).astype(jnp.bfloat16)
    attended = lax.map(one_tile, jnp.arange(NTILES, dtype=jnp.int32)).reshape(TOKENS, HEADS * HD)
    product = jnp.dot(attended, proj_weight, preferred_element_type=jnp.float32)
    return (rows + modulation[2] * product).astype(jnp.bfloat16)
```

```python
import functools
import math

import jax
import jax.numpy as jnp
from jax import lax
from jax.experimental import pallas as pl
from jax.experimental.pallas import tpu as pltpu
from jax.sharding import PartitionSpec as P

HD = 128
TILE = 384
TXT = 256
CHUNKS = ((0, 256), (256, 256), (512, 128), (640, 128))

epsilon = 1e-06
LOG2E = math.log2(math.e)
FACTOR = LOG2E / math.sqrt(HD)

SMEM = pl.BlockSpec(memory_space=pltpu.SMEM)
VMEM = pl.BlockSpec(memory_space=pltpu.VMEM)
NT = (((1,), (1,)), ((), ()))


def rms_norm(values, gain):
    return values * lax.rsqrt(jnp.mean(values * values, axis=-1, keepdims=True) + epsilon) * gain


def project_kernel(count, place_ref, *refs):
    pieces = refs[:count]
    modulation_ref, weight_ref, query_gain_ref, key_gain_ref, query_ref, kv_ref = refs[count:]
    width = pieces[0].shape[1]
    features = width * count
    total = sum(jnp.sum(piece[...].astype(jnp.float32), axis=1, keepdims=True) for piece in pieces)
    average = total / features
    spread = 0.0
    for piece in pieces:
        centred = piece[...].astype(jnp.float32) - average
        spread = spread + jnp.sum(centred * centred, axis=1, keepdims=True)
    scale = lax.rsqrt(spread / features + epsilon)
    projected = 0.0
    for place, piece in enumerate(pieces):
        first = place_ref[place] * width
        if count > 1:
            first = pl.multiple_of(first, width)
        span = pl.ds(first, width)
        centred = piece[...].astype(jnp.float32) - average
        modulated = (
            centred * scale * (1.0 + modulation_ref[1:2, span]) + modulation_ref[0:1, span]
        ).astype(jnp.bfloat16)
        projected = projected + jnp.dot(
            modulated, weight_ref[span, :], preferred_element_type=jnp.float32
        )
    query_ref[...] = rms_norm(projected[:, :HD], query_gain_ref[...]).astype(jnp.bfloat16)
    kv_ref[:, :HD] = rms_norm(projected[:, HD : 2 * HD], key_gain_ref[...]).astype(jnp.bfloat16)
    kv_ref[:, HD:] = projected[:, 2 * HD :].astype(jnp.bfloat16)


def project(places, pieces, blocks, modulation, weight, query_gain, key_gain, rows):
    count = len(pieces)
    specs = [pl.BlockSpec((rows, piece.shape[1]), lambda i, block=block: (block, 0)) for piece, block in zip(pieces, blocks)]
    return pl.pallas_call(
        functools.partial(project_kernel, count),
        grid=(1,),
        out_shape=(
            jax.ShapeDtypeStruct((rows, HD), jnp.bfloat16),
            jax.ShapeDtypeStruct((rows, 2 * HD), jnp.bfloat16),
        ),
        in_specs=[SMEM] + specs + [VMEM] * 4,
        out_specs=(VMEM, VMEM),
        compiler_params=pltpu.CompilerParams(vmem_limit_bytes=32 * 2**20),
        cost_estimate=pl.CostEstimate(
            flops=2 * rows * 3072 * 384, bytes_accessed=rows * 6144 + 2 * 3072 * 384, transcendentals=rows
        ),
    )(places, *pieces, modulation, weight, query_gain, key_gain)


def attend_block(query, shift, keys, values):
    scores = lax.dot_general(query, keys, NT, preferred_element_type=jnp.float32)
    strips = [
        jnp.exp2(scores[:, at : at + HD] * FACTOR - shift) for at in range(0, keys.shape[0], HD)
    ]
    weights = jnp.concatenate(strips, axis=1) if len(strips) > 1 else strips[0]
    product = jnp.dot(weights.astype(jnp.bfloat16), values, preferred_element_type=jnp.float32)
    return sum(strips), product


def segments(start, size):
    out = []
    at = start
    while at < start + size:
        end = min(start + size, (at // TILE + 1) * TILE)
        out.append((at - start, end - at, at // TILE))
        at = end
    return out


def attend_kernel(plan, tiles, first, last, stacked, allow_ref, *refs):
    refs = list(refs)
    queries = [refs.pop(0) for _ in CHUNKS]
    kvs = [refs.pop(0) for _ in plan]
    if first:
        length_ref, text_ref, query_gain_ref, key_gain_ref = [refs.pop(0) for _ in range(4)]
    else:
        shift_in, total_in, accum_in = [refs.pop(0) for _ in range(3)]
    if last:
        out_ref = refs.pop(0)
        total_ref, accum_ref, query_ref = refs
        shift_ref = shift_in
    else:
        shift_ref, total_ref, accum_ref, query_ref = refs
    for (start, size), piece in zip(CHUNKS, queries):
        query_ref[start : start + size, :] = piece[...]
    if first:
        bound = (
            jnp.max(jnp.abs(query_gain_ref[...])) * jnp.max(jnp.abs(key_gain_ref[...])) * (1.02 * HD * FACTOR)
        )
        live = lax.broadcasted_iota(jnp.int32, (TILE, TXT), 1) < length_ref[0]
    for tile in range(tiles):
        rows = slice(tile * TILE, (tile + 1) * TILE)
        if first:
            scores = lax.dot_general(query_ref[rows, :], text_ref[:, :HD], NT, preferred_element_type=jnp.float32)
            scores = jnp.where(live, scores * FACTOR, -jnp.inf)
            top = jnp.maximum(jnp.max(scores, axis=1, keepdims=True), bound)
            weights = jnp.exp2(scores - top)
            shift_ref[rows, :] = jnp.broadcast_to(top, (TILE, HD))
            total_ref[rows, :] = weights[:, :HD] + weights[:, HD:]
            accum_ref[rows, :] = jnp.dot(
                weights.astype(jnp.bfloat16), text_ref[:, HD:], preferred_element_type=jnp.float32
            )
        else:
            if not last:
                shift_ref[rows, :] = shift_in[rows, :]
            total_ref[rows, :] = total_in[rows, :]
            accum_ref[rows, :] = accum_in[rows, :]
        for (source, start, size), kv in zip(plan, kvs):
            for at, length, slot in segments(start, size):

                def work(source, keys, values, rows=rows, tile=tile, slot=slot):
                    @pl.when(allow_ref[tile, source * tiles + slot] > 0)
                    def _():
                        total, product = attend_block(query_ref[rows, :], shift_ref[rows, :], keys(), values())
                        total_ref[rows, :] += total
                        accum_ref[rows, :] += product

                span = slice(at, at + length)
                if stacked:

                    def step(source, carry, kv=kv, span=span, work=work):
                        work(source, lambda: kv[source, span, :HD], lambda: kv[source, span, HD:])
                        return carry

                    lax.fori_loop(0, kv.shape[0], step, 0)
                else:
                    work(source, lambda: kv[span, :HD], lambda: kv[span, HD:])
        if last:
            total = jnp.sum(total_ref[rows, :], axis=1, keepdims=True)
            out_ref[rows, :] = (accum_ref[rows, :] / total).astype(jnp.bfloat16)


def attend(plan, kvs, allow, queries, tiles, start=None, state=None, last=False, stacked=False):
    rows = tiles * TILE
    first = state is None
    extra = start if first else state
    part = jax.ShapeDtypeStruct((rows, HD), jnp.float32)
    scratch = [pltpu.VMEM((rows, HD), jnp.bfloat16)]
    if last:
        out_shape = jax.ShapeDtypeStruct((rows, HD), jnp.bfloat16)
        scratch = [pltpu.VMEM((rows, HD), jnp.float32)] * 2 + scratch
    else:
        out_shape = (part,) * 3
    keys = sum(kv.size // (2 * HD) for kv in kvs) + (TXT if first else 0)
    return pl.pallas_call(
        functools.partial(attend_kernel, plan, tiles, first, last, stacked),
        out_shape=out_shape,
        in_specs=[SMEM] + [VMEM] * (len(queries) + len(kvs)) + ([SMEM] if first else []) + [VMEM] * 3,
        out_specs=VMEM if last else (VMEM,) * 3,
        scratch_shapes=scratch,
        compiler_params=pltpu.CompilerParams(vmem_limit_bytes=32 * 2**20),
        cost_estimate=pl.CostEstimate(
            flops=4 * rows * keys * HD, bytes_accessed=rows * HD * 14 + keys * HD * 4, transcendentals=rows * keys
        ),
    )(allow, *queries, *kvs, *extra)


def merge_kernel(count, place_ref, *refs):
    pieces = refs[:count]
    weight_ref, latents_ref, gate_ref, out_ref = refs[count:]
    depth = pieces[0].shape[1]
    product = 0.0
    for place, piece in enumerate(pieces):
        first = place_ref[place] * depth
        if count > 1:
            first = pl.multiple_of(first, depth)
        product = product + jnp.dot(
            piece[...], weight_ref[pl.ds(first, depth), :], preferred_element_type=jnp.float32
        )
    out_ref[...] = (latents_ref[...].astype(jnp.float32) + gate_ref[...] * product).astype(jnp.bfloat16)


def merge(places, pieces, weight, latents, gate):
    rows, width = latents.shape
    block = 256
    return pl.pallas_call(
        functools.partial(merge_kernel, len(pieces)),
        grid=(rows // block,),
        out_shape=jax.ShapeDtypeStruct((rows, width), jnp.bfloat16),
        in_specs=[SMEM]
        + [pl.BlockSpec((block, piece.shape[1]), lambda i: (i, 0)) for piece in pieces]
        + [
            pl.BlockSpec(weight.shape, lambda i: (0, 0)),
            pl.BlockSpec((block, width), lambda i: (i, 0)),
            pl.BlockSpec(gate.shape, lambda i: (0, 0)),
        ],
        out_specs=pl.BlockSpec((block, width), lambda i: (i, 0)),
        compiler_params=pltpu.CompilerParams(vmem_limit_bytes=32 * 2**20),
        cost_estimate=pl.CostEstimate(
            flops=2 * rows * width * weight.shape[0],
            bytes_accessed=rows * width * 4 + weight.size * 2 + rows * weight.shape[0] * 2,
            transcendentals=0,
        ),
    )(places, *pieces, weight, latents, gate)


def shifted(values, axis, size, by):
    return lax.ppermute(values, axis, [(at, (at + by) % size) for at in range(size)])


def body(
    heads_size,
    cfg_size,
    tiles_size,
    latents,
    modulation,
    qkv_weight,
    query_gain,
    key_gain,
    text_kv,
    text_len,
    tile_ids,
    windows,
    proj_weight,
):
    pairs = heads_size == 2 and cfg_size == 2
    stacked = tiles_size > 4
    per_dev = tile_ids.shape[0]
    width = latents.shape[1]
    me = lax.axis_index(("heads", "cfg"))
    query_gain = query_gain[None, :]
    key_gain = key_gain[None, :]

    if pairs:
        across = [shifted(latents[start : start + size], "heads", 2, 1) for start, size in CHUNKS]
        beside = shifted(latents, "cfg", 2, 1)
        places = jnp.stack([me, me ^ 1, me ^ 2, me ^ 3]).astype(jnp.int32)
    else:
        gathered = lax.all_gather(latents, ("heads", "cfg"), axis=1, tiled=True)
        places = jnp.zeros((1,), jnp.int32)

    if stacked:
        ids = lax.all_gather(tile_ids, "tiles", axis=0, tiled=True)
    else:
        ids = jnp.concatenate([tile_ids] + [shifted(tile_ids, "tiles", tiles_size, by) for by in range(1, tiles_size)])
    allow = jnp.any(windows[tile_ids][:, :, None] == ids[None, None, :], axis=1).astype(jnp.int32)

    queries = []
    kvs = []
    remote = []
    for number, (start, size) in enumerate(CHUNKS):
        block = start // size
        if pairs:
            far = across[number]
            pieces = [latents, beside, far, shifted(far, "cfg", 2, 1)]
            blocks = [block, block, 0, 0]
        else:
            pieces = [gathered]
            blocks = [block]
        query, kv = project(places, pieces, blocks, modulation, qkv_weight, query_gain, key_gain, size)
        queries.append(query)
        kvs.append(kv)
        if stacked:
            remote.append([lax.all_gather(kv, "tiles", axis=0)])
        else:
            remote.append([shifted(kv, "tiles", tiles_size, by) for by in range(1, tiles_size)])

    begin = (text_len, text_kv, query_gain, key_gain)

    def plan_of(numbers):
        plan, arrays = [], []
        for number in numbers:
            for by, array in enumerate(remote[number]):
                plan.append((by + 1,) + CHUNKS[number])
                arrays.append(array)
        return plan, arrays

    own_plan, own = ([], []) if stacked else ([(0,) + chunk for chunk in CHUNKS], kvs)
    state = attend(own_plan, own, allow, queries, per_dev, start=begin)
    final = len(CHUNKS) - 1
    plan, arrays = plan_of(range(final - 1))
    state = attend(plan, arrays, allow, queries, per_dev, state=state, stacked=stacked)
    plan, arrays = plan_of([final - 1])
    state = attend(plan, arrays, allow, queries, per_dev, state=state, stacked=stacked)
    plan, arrays = plan_of([final])
    attended = attend(plan, arrays, allow, queries, per_dev, state=state, last=True, stacked=stacked)

    if pairs:
        far = shifted(attended, "heads", 2, 1)
        pieces = [attended, shifted(attended, "cfg", 2, 1), far, shifted(far, "cfg", 2, 1)]
    else:
        pieces = [lax.all_gather(attended, ("heads", "cfg"), axis=1, tiled=True)]
    gate = lax.dynamic_slice_in_dim(modulation[2:3], me * width, width, 1)
    return merge(places, pieces, proj_weight, latents, gate)


def solution(mesh):
    in_specs = (
        P(("groups", "tiles"), ("heads", "cfg")),
        P("groups", None),
        P(None, ("heads", "cfg")),
        P(),
        P(),
        P("groups", ("heads", "cfg")),
        P("groups"),
        P(("groups", "tiles")),
        P("groups", None),
        P(None, ("heads", "cfg")),
    )
    out_specs = P(("groups", "tiles"), ("heads", "cfg"))
    run = functools.partial(body, mesh.shape["heads"], mesh.shape["cfg"], mesh.shape["tiles"])
    return jax.shard_map(run, mesh=mesh, in_specs=in_specs, out_specs=out_specs, check_vma=False)
```

```python
import functools
import math

import jax
import jax.numpy as jnp
from jax import lax
from jax.experimental import pallas as pl
from jax.experimental.pallas import tpu as pltpu
from jax.sharding import PartitionSpec as P

HD = 128
TILE = 384
TXT = 256
CHUNKS = ((0, 128), (128, 256), (384, 256), (640, 128))
LABEL_ROWS = 16

epsilon = 1e-06
LOG2E = math.log2(math.e)
FACTOR = LOG2E / math.sqrt(HD)

SMEM = pl.BlockSpec(memory_space=pltpu.SMEM)
VMEM = pl.BlockSpec(memory_space=pltpu.VMEM)
HBM = pl.BlockSpec(memory_space=pltpu.HBM)
PROJECT_LIMIT = 24 * 2**20
ATTEND_LIMIT = 16 * 2**20
MERGE_LIMIT = 16 * 2**20
NT = (((1,), (1,)), ((), ()))


def rms_norm(values, gain):
    return values * lax.rsqrt(jnp.mean(values * values, axis=-1, keepdims=True) + epsilon) * gain


def project_kernel(count, starts, rows, place_ref, ids_ref, *refs):
    sources = refs[:count]
    modulation_ref, query_gain_ref, key_gain_ref, weight_ref = refs[count : count + 4]
    query_ref, kv_ref, pieces_ref, piece_sem = refs[count + 4 :]
    width = sources[0].shape[1]
    features = width * count
    spans = []
    piece_copies = []
    for place, (source, start) in enumerate(zip(sources, starts)):
        first = place_ref[place] * width
        if count > 1:
            first = pl.multiple_of(first, width)
        spans.append(pl.ds(first, width))
        piece_copies.append(
            pltpu.make_async_copy(source.at[start : start + rows, :], pieces_ref.at[place], piece_sem.at[place])
        )
    for copy in piece_copies:
        copy.start()
    total = 0.0
    for place, copy in enumerate(piece_copies):
        copy.wait()
        total = total + jnp.sum(pieces_ref[place].astype(jnp.float32), axis=1, keepdims=True)
    average = total / features
    spread = 0.0
    for place in range(count):
        centred = pieces_ref[place].astype(jnp.float32) - average
        spread = spread + jnp.sum(centred * centred, axis=1, keepdims=True)
    scale = lax.rsqrt(spread / features + epsilon)
    projected = 0.0
    for place, span in enumerate(spans):
        centred = pieces_ref[place].astype(jnp.float32) - average
        modulated = (
            centred * scale * (1.0 + modulation_ref[1:2, span]) + modulation_ref[0:1, span]
        ).astype(jnp.bfloat16)
        projected = projected + jnp.dot(modulated, weight_ref[span, :], preferred_element_type=jnp.float32)
    query_ref[...] = rms_norm(projected[:, :HD], query_gain_ref[...]).astype(jnp.bfloat16)
    kv_ref[:rows, :HD] = rms_norm(projected[:, HD : 2 * HD], key_gain_ref[...]).astype(jnp.bfloat16)
    kv_ref[:rows, HD:] = projected[:, 2 * HD :].astype(jnp.bfloat16)
    labels = kv_ref.shape[0] - rows
    if labels:
        lane = lax.broadcasted_iota(jnp.int32, (labels, 2 * HD), 1)
        label = jnp.full((labels, 2 * HD), ids_ref[0], jnp.int32)
        for slot in range(1, ids_ref.shape[0]):
            label = jnp.where(lane == slot, ids_ref[slot], label)
        kv_ref[rows:, :] = label.astype(jnp.float32).astype(jnp.bfloat16)


def project(places, ids, pieces, starts, modulation, weight, query_gain, key_gain, rows, labels):
    count = len(pieces)
    width = pieces[0].shape[1]
    return pl.pallas_call(
        functools.partial(project_kernel, count, starts, rows),
        out_shape=(
            jax.ShapeDtypeStruct((rows, HD), jnp.bfloat16),
            jax.ShapeDtypeStruct((rows + labels, 2 * HD), jnp.bfloat16),
        ),
        in_specs=[SMEM] * 2 + [HBM] * count + [VMEM] * 4,
        out_specs=(VMEM, VMEM),
        scratch_shapes=[
            pltpu.VMEM((count, rows, width), jnp.bfloat16),
            pltpu.SemaphoreType.DMA((count,)),
        ],
        compiler_params=pltpu.CompilerParams(vmem_limit_bytes=PROJECT_LIMIT),
        cost_estimate=pl.CostEstimate(flops=2 * rows * 3072 * 384, bytes_accessed=rows * 6144 + 2 * 3072 * 384, transcendentals=rows),
    )(places, ids, *pieces, modulation, query_gain, key_gain, weight)


def attend_block(query, shift, keys, values):
    scores = lax.dot_general(query, keys, NT, preferred_element_type=jnp.float32)
    strips = [
        jnp.exp2(scores[:, at : at + HD] * FACTOR - shift) for at in range(0, keys.shape[0], HD)
    ]
    weights = jnp.concatenate(strips, axis=1) if len(strips) > 1 else strips[0]
    product = jnp.dot(weights.astype(jnp.bfloat16), values, preferred_element_type=jnp.float32)
    return sum(strips), product


def segments(start, size):
    out = []
    at = start
    while at < start + size:
        end = min(start + size, (at // TILE + 1) * TILE)
        out.append((at - start, end - at, at // TILE))
        at = end
    return out


def attend_kernel(plan, tiles, first, last, stacked, ids_ref, own_ref, windows_ref, *refs):
    refs = list(refs)
    queries = [refs.pop(0) for _ in CHUNKS]
    kvs = [refs.pop(0) for _ in plan]
    if first:
        length_ref, text_ref, query_gain_ref, key_gain_ref = [refs.pop(0) for _ in range(4)]
    else:
        shift_in, total_in, accum_in = [refs.pop(0) for _ in range(3)]
    if last:
        out_ref = refs.pop(0)
        total_ref, accum_ref, query_ref = refs
        shift_ref = shift_in
    else:
        shift_ref, total_ref, accum_ref, query_ref = refs
    for (start, size), piece in zip(CHUNKS, queries):
        query_ref[start : start + size, :] = piece[...]
    if first:
        bound = (
            jnp.max(jnp.abs(query_gain_ref[...])) * jnp.max(jnp.abs(key_gain_ref[...])) * (1.02 * HD * FACTOR)
        )
        live = lax.broadcasted_iota(jnp.int32, (TILE, TXT), 1) < length_ref[0]
    for tile in range(tiles):
        rows = slice(tile * TILE, (tile + 1) * TILE)
        own = own_ref[tile]
        reach = 0
        for entry in range(windows_ref.shape[1]):
            reach = reach | (1 << windows_ref[own, entry])
        if first:
            scores = lax.dot_general(query_ref[rows, :], text_ref[:, :HD], NT, preferred_element_type=jnp.float32)
            scores = jnp.where(live, scores * FACTOR, -jnp.inf)
            top = jnp.maximum(jnp.max(scores, axis=1, keepdims=True), bound)
            weights = jnp.exp2(scores - top)
            shift_ref[rows, :] = jnp.broadcast_to(top, (TILE, HD))
            total_ref[rows, :] = weights[:, :HD] + weights[:, HD:]
            accum_ref[rows, :] = jnp.dot(
                weights.astype(jnp.bfloat16), text_ref[:, HD:], preferred_element_type=jnp.float32
            )
        else:
            if not last:
                shift_ref[rows, :] = shift_in[rows, :]
            total_ref[rows, :] = total_in[rows, :]
            accum_ref[rows, :] = accum_in[rows, :]
        for (source, start, size), kv in zip(plan, kvs):
            for at, length, slot in segments(start, size):

                def work(source, keys, values, rows=rows, reach=reach, slot=slot):
                    @pl.when(((reach >> ids_ref[source * tiles + slot]) & 1) > 0)
                    def _():
                        total, product = attend_block(query_ref[rows, :], shift_ref[rows, :], keys(), values())
                        total_ref[rows, :] += total
                        accum_ref[rows, :] += product

                span = slice(at, at + length)
                if stacked:

                    def step(source, carry, kv=kv, span=span, work=work):
                        work(source, lambda: kv[source, span, :HD], lambda: kv[source, span, HD:])
                        return carry

                    lax.fori_loop(0, kv.shape[0], step, 0)
                else:
                    work(source, lambda: kv[span, :HD], lambda: kv[span, HD:])
        if last:
            total = jnp.sum(total_ref[rows, :], axis=1, keepdims=True)
            out_ref[rows, :] = (accum_ref[rows, :] / total).astype(jnp.bfloat16)


def attend(plan, kvs, ids, own_ids, windows, queries, tiles, start=None, state=None, last=False, stacked=False):
    rows = tiles * TILE
    first = state is None
    extra = start if first else state
    part = jax.ShapeDtypeStruct((rows, HD), jnp.float32)
    scratch = [pltpu.VMEM((rows, HD), jnp.bfloat16)]
    if last:
        out_shape = jax.ShapeDtypeStruct((rows, HD), jnp.bfloat16)
        scratch = [pltpu.VMEM((rows, HD), jnp.float32)] * 2 + scratch
    else:
        out_shape = (part,) * 3
    keys = sum(kv.size // (2 * HD) for kv in kvs) + (TXT if first else 0)
    return pl.pallas_call(
        functools.partial(attend_kernel, plan, tiles, first, last, stacked),
        out_shape=out_shape,
        in_specs=[SMEM] * 3 + [VMEM] * (len(queries) + len(kvs)) + ([SMEM] if first else []) + [VMEM] * 3,
        out_specs=VMEM if last else (VMEM,) * 3,
        scratch_shapes=scratch,
        compiler_params=pltpu.CompilerParams(vmem_limit_bytes=ATTEND_LIMIT),
        cost_estimate=pl.CostEstimate(flops=4 * rows * keys * HD, bytes_accessed=rows * HD * 14 + keys * HD * 4, transcendentals=rows * keys),
    )(ids, own_ids, windows, *queries, *kvs, *extra)


def merge_kernel(count, place_ref, *refs):
    pieces = refs[:count]
    weight_ref, latents_ref, gate_ref, out_ref = refs[count:]
    depth = pieces[0].shape[1]
    width = latents_ref.shape[1]
    if count > 1:
        gate = gate_ref[2:3, pl.ds(pl.multiple_of(place_ref[0] * width, width), width)]
    else:
        gate = gate_ref[...]
    product = 0.0
    for place, piece in enumerate(pieces):
        first = place_ref[place] * depth
        if count > 1:
            first = pl.multiple_of(first, depth)
        product = product + jnp.dot(
            piece[...], weight_ref[pl.ds(first, depth), :], preferred_element_type=jnp.float32
        )
    out_ref[...] = (latents_ref[...].astype(jnp.float32) + gate * product).astype(jnp.bfloat16)


def merge(places, pieces, weight, latents, gate):
    rows, width = latents.shape
    block = 256
    return pl.pallas_call(
        functools.partial(merge_kernel, len(pieces)),
        grid=(rows // block,),
        out_shape=jax.ShapeDtypeStruct((rows, width), jnp.bfloat16),
        in_specs=[SMEM]
        + [pl.BlockSpec((block, piece.shape[1]), lambda i: (i, 0)) for piece in pieces]
        + [
            pl.BlockSpec(weight.shape, lambda i: (0, 0)),
            pl.BlockSpec((block, width), lambda i: (i, 0)),
            pl.BlockSpec(gate.shape, lambda i: (0, 0)),
        ],
        out_specs=pl.BlockSpec((block, width), lambda i: (i, 0)),
        compiler_params=pltpu.CompilerParams(vmem_limit_bytes=MERGE_LIMIT),
        cost_estimate=pl.CostEstimate(
            flops=2 * rows * width * weight.shape[0],
            bytes_accessed=rows * width * 4 + weight.size * 2 + rows * weight.shape[0] * 2,
            transcendentals=0,
        ),
    )(places, *pieces, weight, latents, gate)


def shifted(values, axis, size, by):
    return lax.ppermute(values, axis, [(at, (at + by) % size) for at in range(size)])


def body(
    heads_size,
    cfg_size,
    tiles_size,
    latents,
    modulation,
    qkv_weight,
    query_gain,
    key_gain,
    text_kv,
    text_len,
    tile_ids,
    windows,
    proj_weight,
):
    pairs = heads_size == 2 and cfg_size == 2
    stacked = tiles_size > 4
    per_dev = tile_ids.shape[0]
    width = latents.shape[1]
    me = lax.axis_index(("heads", "cfg"))
    query_gain = query_gain[None, :]
    key_gain = key_gain[None, :]

    if pairs:
        across = [shifted(latents[start : start + size], "heads", 2, 1) for start, size in CHUNKS]
        beside = shifted(latents, "cfg", 2, 1)
        places = jnp.stack([me, me ^ 1, me ^ 2, me ^ 3]).astype(jnp.int32)
    else:
        gathered = lax.all_gather(latents, ("heads", "cfg"), axis=1, tiled=True)
        places = jnp.zeros((1,), jnp.int32)

    queries = []
    kvs = []
    remote = []
    for number, (start, size) in enumerate(CHUNKS):
        if pairs:
            far = across[number]
            if number:
                far, unused = lax.optimization_barrier((far, kvs[-1]))
            pieces = [latents, beside, far, shifted(far, "cfg", 2, 1)]
            starts = [start, start, 0, 0]
        else:
            pieces = [gathered]
            starts = [start]
        query, kv = project(
            places, tile_ids, pieces, starts, modulation, qkv_weight, query_gain, key_gain, size, 0 if number else LABEL_ROWS
        )
        queries.append(query)
        kvs.append(kv)
        if stacked:
            remote.append([lax.all_gather(kv, "tiles", axis=0)])
        else:
            remote.append([shifted(kv, "tiles", tiles_size, by) for by in range(1, tiles_size)])

    labels = [array[..., CHUNKS[0][1], :per_dev].reshape(-1).astype(jnp.int32) for array in remote[0]]
    ids = labels[0] if stacked else jnp.concatenate([tile_ids] + labels)
    begin = (text_len, text_kv, query_gain, key_gain)

    def plan_of(numbers):
        plan, arrays = [], []
        for number in numbers:
            for by, array in enumerate(remote[number]):
                plan.append((by + 1,) + CHUNKS[number])
                arrays.append(array)
        return plan, arrays

    own_plan, own = ([], []) if stacked else ([(0,) + chunk for chunk in CHUNKS], kvs)
    state = attend(own_plan, own, tile_ids, tile_ids, windows, queries, per_dev, start=begin)
    final = len(CHUNKS) - 1
    plan, arrays = plan_of(range(final - 1))
    state = attend(plan, arrays, ids, tile_ids, windows, queries, per_dev, state=state, stacked=stacked)
    plan, arrays = plan_of([final - 1])
    state = attend(plan, arrays, ids, tile_ids, windows, queries, per_dev, state=state, stacked=stacked)
    plan, arrays = plan_of([final])
    attended = attend(plan, arrays, ids, tile_ids, windows, queries, per_dev, state=state, last=True, stacked=stacked)

    if pairs:
        far = shifted(attended, "heads", 2, 1)
        pieces = [attended, shifted(attended, "cfg", 2, 1), far, shifted(far, "cfg", 2, 1)]
    else:
        pieces = [lax.all_gather(attended, ("heads", "cfg"), axis=1, tiled=True)]
    gate = modulation if pairs else lax.dynamic_slice_in_dim(modulation[2:3], me * width, width, 1)
    return merge(places, pieces, proj_weight, latents, gate)


def solution(mesh):
    in_specs = (
        P(("groups", "tiles"), ("heads", "cfg")),
        P("groups", None),
        P(None, ("heads", "cfg")),
        P(),
        P(),
        P("groups", ("heads", "cfg")),
        P("groups"),
        P(("groups", "tiles")),
        P("groups", None),
        P(None, ("heads", "cfg")),
    )
    out_specs = P(("groups", "tiles"), ("heads", "cfg"))
    run = functools.partial(body, mesh.shape["heads"], mesh.shape["cfg"], mesh.shape["tiles"])
    return jax.shard_map(run, mesh=mesh, in_specs=in_specs, out_specs=out_specs, check_vma=False)
```

```python
import functools
import math

import jax
import jax.numpy as jnp
from jax import lax
from jax.experimental import pallas as pl
from jax.experimental.pallas import tpu as pltpu
from jax.sharding import PartitionSpec as P

HD = 128
TILE = 384
TXT = 256
CHUNKS = ((0, 128), (128, 256), (384, 384))
LABEL_ROWS = 16

epsilon = 1e-06
LOG2E = math.log2(math.e)
FACTOR = LOG2E / math.sqrt(HD)

SMEM = pl.BlockSpec(memory_space=pltpu.SMEM)
VMEM = pl.BlockSpec(memory_space=pltpu.VMEM)
HBM = pl.BlockSpec(memory_space=pltpu.HBM)
ANY = pl.BlockSpec(memory_space=pl.ANY)
PROJECT_LIMIT = 24 * 2**20
ATTEND_LIMIT = 16 * 2**20
MERGE_LIMIT = 16 * 2**20
NT = (((1,), (1,)), ((), ()))


def rms_norm(values, gain):
    return values * lax.rsqrt(jnp.mean(values * values, axis=-1, keepdims=True) + epsilon) * gain


def project_kernel(count, after, starts, rows, place_ref, ids_ref, *refs):
    sources = refs[:count]
    refs = refs[:count] + refs[count + after :]
    modulation_ref, query_gain_ref, key_gain_ref, weight_ref = refs[count : count + 4]
    query_ref, kv_ref, pieces_ref, piece_sem = refs[count + 4 :]
    width = sources[0].shape[1]
    features = width * count
    spans = []
    piece_copies = []
    for place, (source, start) in enumerate(zip(sources, starts)):
        first = place_ref[place] * width
        if count > 1:
            first = pl.multiple_of(first, width)
        spans.append(pl.ds(first, width))
        piece_copies.append(
            pltpu.make_async_copy(source.at[start : start + rows, :], pieces_ref.at[place], piece_sem.at[place])
        )
    for copy in piece_copies:
        copy.start()
    total = 0.0
    for place, copy in enumerate(piece_copies):
        copy.wait()
        total = total + jnp.sum(pieces_ref[place].astype(jnp.float32), axis=1, keepdims=True)
    average = total / features
    spread = 0.0
    for place in range(count):
        centred = pieces_ref[place].astype(jnp.float32) - average
        spread = spread + jnp.sum(centred * centred, axis=1, keepdims=True)
    scale = lax.rsqrt(spread / features + epsilon)
    projected = 0.0
    for place, span in enumerate(spans):
        centred = pieces_ref[place].astype(jnp.float32) - average
        modulated = (
            centred * scale * (1.0 + modulation_ref[1:2, span]) + modulation_ref[0:1, span]
        ).astype(jnp.bfloat16)
        projected = projected + jnp.dot(modulated, weight_ref[span, :], preferred_element_type=jnp.float32)
    query_ref[...] = rms_norm(projected[:, :HD], query_gain_ref[...]).astype(jnp.bfloat16)
    kv_ref[:rows, :HD] = rms_norm(projected[:, HD : 2 * HD], key_gain_ref[...]).astype(jnp.bfloat16)
    kv_ref[:rows, HD:] = projected[:, 2 * HD :].astype(jnp.bfloat16)
    labels = kv_ref.shape[0] - rows
    if labels:
        lane = lax.broadcasted_iota(jnp.int32, (labels, 2 * HD), 1)
        label = jnp.full((labels, 2 * HD), ids_ref[0], jnp.int32)
        for slot in range(1, ids_ref.shape[0]):
            label = jnp.where(lane == slot, ids_ref[slot], label)
        kv_ref[rows:, :] = label.astype(jnp.float32).astype(jnp.bfloat16)


def preload_kernel(weight_ref, out_ref, sem):
    copy = pltpu.make_async_copy(weight_ref, out_ref, sem)
    copy.start()
    copy.wait()


def preload(weight):
    return pl.pallas_call(
        preload_kernel,
        out_shape=jax.ShapeDtypeStruct(weight.shape, weight.dtype),
        in_specs=[HBM],
        out_specs=VMEM,
        scratch_shapes=[pltpu.SemaphoreType.DMA],
        compiler_params=pltpu.CompilerParams(vmem_limit_bytes=ATTEND_LIMIT),
        cost_estimate=pl.CostEstimate(flops=0, bytes_accessed=4096, transcendentals=0),
    )(weight)


def project(places, ids, pieces, after, starts, modulation, weight, query_gain, key_gain, rows, labels):
    count = len(pieces)
    width = pieces[0].shape[1]
    return pl.pallas_call(
        functools.partial(project_kernel, count, len(after), starts, rows),
        out_shape=(
            jax.ShapeDtypeStruct((rows, HD), jnp.bfloat16),
            jax.ShapeDtypeStruct((rows + labels, 2 * HD), jnp.bfloat16),
        ),
        in_specs=[SMEM] * 2 + [HBM] * count + [ANY] * len(after) + [VMEM] * 4,
        out_specs=(VMEM, VMEM),
        scratch_shapes=[
            pltpu.VMEM((count, rows, width), jnp.bfloat16),
            pltpu.SemaphoreType.DMA((count,)),
        ],
        compiler_params=pltpu.CompilerParams(vmem_limit_bytes=PROJECT_LIMIT),
        cost_estimate=pl.CostEstimate(flops=rows, bytes_accessed=rows, transcendentals=rows),
    )(places, ids, *pieces, *after, modulation, query_gain, key_gain, weight)


def attend_block(query, shift, keys, values):
    scores = lax.dot_general(query, keys, NT, preferred_element_type=jnp.float32)
    strips = [
        jnp.exp2(scores[:, at : at + HD] * FACTOR - shift) for at in range(0, keys.shape[0], HD)
    ]
    weights = jnp.concatenate(strips, axis=1) if len(strips) > 1 else strips[0]
    product = jnp.dot(weights.astype(jnp.bfloat16), values, preferred_element_type=jnp.float32)
    return sum(strips), product


def segments(start, size):
    out = []
    at = start
    while at < start + size:
        end = min(start + size, (at // TILE + 1) * TILE)
        out.append((at - start, end - at, at // TILE))
        at = end
    return out


def attend_kernel(starts, plan, tiles, begin, held, last, stacked, ids_ref, own_ref, windows_ref, *refs):
    refs = list(refs)
    queries = [refs.pop(0) for _ in starts]
    kvs = [refs.pop(0) for _ in plan]
    if begin:
        length_ref, text_ref, query_gain_ref, key_gain_ref = [refs.pop(0) for _ in range(4)]
    if held:
        shift_in, total_in, accum_in = [refs.pop(0) for _ in range(3)]
    if last:
        out_ref = refs.pop(0)
    shift_ref, total_ref, accum_ref, query_ref = refs
    for start, piece in zip(starts, queries):
        query_ref[start : start + piece.shape[0], :] = piece[...]
    if begin:
        bound = (
            jnp.max(jnp.abs(query_gain_ref[...])) * jnp.max(jnp.abs(key_gain_ref[...])) * (1.02 * HD * FACTOR)
        )
        live = lax.broadcasted_iota(jnp.int32, (TILE, TXT), 1) < length_ref[0]
    for tile in sorted(begin + held):
        rows = slice(tile * TILE, (tile + 1) * TILE)
        if tile in begin:
            scores = lax.dot_general(query_ref[rows, :], text_ref[:, :HD], NT, preferred_element_type=jnp.float32)
            scores = jnp.where(live, scores * FACTOR, -jnp.inf)
            top = jnp.maximum(jnp.max(scores, axis=1, keepdims=True), bound)
            weights = jnp.exp2(scores - top)
            shift_ref[rows, :] = jnp.broadcast_to(top, (TILE, HD))
            total_ref[rows, :] = weights[:, :HD] + weights[:, HD:]
            accum_ref[rows, :] = jnp.dot(
                weights.astype(jnp.bfloat16), text_ref[:, HD:], preferred_element_type=jnp.float32
            )
        else:
            shift_ref[rows, :] = shift_in[rows, :]
            total_ref[rows, :] = total_in[rows, :]
            accum_ref[rows, :] = accum_in[rows, :]
        own = own_ref[tile]
        reach = 0
        for entry in range(windows_ref.shape[1]):
            reach = reach | (1 << windows_ref[own, entry])
        groups = {}
        for number, (source, start, size, wanted) in enumerate(plan):
            if tile in wanted:
                for at, length, slot in segments(start, size):
                    groups.setdefault((source, slot), []).append((number, slice(at, at + length)))
        for (source, slot), blocks in groups.items():

            def work(source, view, rows=rows, reach=reach, slot=slot, blocks=blocks):
                @pl.when(((reach >> ids_ref[source * tiles + slot]) & 1) > 0)
                def _():
                    parts = [
                        attend_block(
                            query_ref[rows, :], shift_ref[rows, :], view(number)[span, :HD], view(number)[span, HD:]
                        )
                        for number, span in blocks
                    ]
                    total_ref[rows, :] += sum(total for total, product in parts)
                    accum_ref[rows, :] += sum(product for total, product in parts)

            if stacked:

                def step(source, carry, work=work):
                    work(source, lambda number: kvs[number].at[source])
                    return carry

                lax.fori_loop(0, kvs[0].shape[0], step, 0)
            else:
                work(source, lambda number: kvs[number])
        if last:
            total = jnp.sum(total_ref[rows, :], axis=1, keepdims=True)
            out_ref[rows, :] = (accum_ref[rows, :] / total).astype(jnp.bfloat16)


def attend(tokens, queries, pieces, begin, held, start=(), state=(), last=False, stacked=False):
    ids, own_ids, windows = tokens
    tiles = own_ids.shape[0]
    rows = tiles * TILE
    part = jax.ShapeDtypeStruct((rows, HD), jnp.float32)
    scratch = [pltpu.VMEM((rows, HD), jnp.bfloat16)]
    if last:
        out_shape = jax.ShapeDtypeStruct((rows, HD), jnp.bfloat16)
        scratch = [pltpu.VMEM((rows, HD), jnp.float32)] * 3 + scratch
    else:
        out_shape = (part,) * 3
    keys = sum(piece[0].size // (2 * HD) for piece in pieces)
    extra = (tuple(start) if begin else ()) + tuple(state)
    return pl.pallas_call(
        functools.partial(
            attend_kernel, [at for at, array in queries], [piece[1:] for piece in pieces], tiles, begin, held, last, stacked
        ),
        out_shape=out_shape,
        in_specs=[SMEM] * 3
        + [VMEM] * (len(queries) + len(pieces))
        + ([SMEM] + [VMEM] * 3 if begin else [])
        + [VMEM] * len(state),
        out_specs=VMEM if last else (VMEM,) * 3,
        scratch_shapes=scratch,
        compiler_params=pltpu.CompilerParams(vmem_limit_bytes=ATTEND_LIMIT),
        cost_estimate=pl.CostEstimate(flops=rows * keys, bytes_accessed=rows * HD, transcendentals=rows),
    )(ids, own_ids, windows, *[array for at, array in queries], *[piece[0] for piece in pieces], *extra)


def merge_kernel(count, place_ref, *refs):
    pieces = refs[:count]
    weight_ref, latents_ref, gate_ref, out_ref, joined_ref = refs[count:]
    depth = pieces[0].shape[1]
    width = latents_ref.shape[1]
    if count > 1:
        gate = gate_ref[2:3, pl.ds(pl.multiple_of(place_ref[0] * width, width), width)]
        for place, piece in enumerate(pieces):
            joined_ref[:, pl.ds(pl.multiple_of(place_ref[place] * depth, depth), depth)] = piece[...]
        attended = joined_ref[...]
    else:
        gate = gate_ref[...]
        attended = pieces[0][...]
    product = jnp.dot(attended, weight_ref[...], preferred_element_type=jnp.float32)
    out_ref[...] = (latents_ref[...].astype(jnp.float32) + gate * product).astype(jnp.bfloat16)


def merge(places, pieces, weight, latents, gate):
    rows, width = latents.shape
    block = 256
    return pl.pallas_call(
        functools.partial(merge_kernel, len(pieces)),
        grid=(rows // block,),
        out_shape=jax.ShapeDtypeStruct((rows, width), jnp.bfloat16),
        in_specs=[SMEM]
        + [pl.BlockSpec((block, piece.shape[1]), lambda i: (i, 0)) for piece in pieces]
        + [
            pl.BlockSpec(weight.shape, lambda i: (0, 0)),
            pl.BlockSpec((block, width), lambda i: (i, 0)),
            pl.BlockSpec(gate.shape, lambda i: (0, 0)),
        ],
        out_specs=pl.BlockSpec((block, width), lambda i: (i, 0)),
        scratch_shapes=[pltpu.VMEM((block, len(pieces) * pieces[0].shape[1]), jnp.bfloat16)],
        compiler_params=pltpu.CompilerParams(vmem_limit_bytes=MERGE_LIMIT),
        cost_estimate=pl.CostEstimate(
            flops=2 * rows * width * weight.shape[0],
            bytes_accessed=rows * width * 4 + weight.size * 2 + rows * weight.shape[0] * 2,
            transcendentals=0,
        ),
    )(places, *pieces, weight, latents, gate)


def shifted(values, axis, size, by):
    return lax.ppermute(values, axis, [(at, (at + by) % size) for at in range(size)])


LINE = 4


NEAR = [(0, 1), (1, 0), (2, 3), (3, 2)]
AWAY = [(0, 2), (1, 3), (2, 0), (3, 1)]


def ordered(values, *before):
    return lax.optimization_barrier((values, *before))[0]


def body(
    heads_size,
    cfg_size,
    tiles_size,
    latents,
    modulation,
    qkv_weight,
    query_gain,
    key_gain,
    text_kv,
    text_len,
    tile_ids,
    windows,
    proj_weight,
):
    pairs = heads_size == 2 and cfg_size == 2
    stacked = tiles_size != LINE
    per_dev = tile_ids.shape[0]
    width = latents.shape[1]
    me = lax.axis_index(("heads", "cfg"))
    query_gain = query_gain[None, :]
    key_gain = key_gain[None, :]

    begin = (text_len, text_kv, query_gain, key_gain)
    everyone = list(range(per_dev))

    if pairs:
        parts = [latents[: CHUNKS[0][1]]]
        rest = ordered(latents, parts[0])
        parts += [rest[start : start + size] for start, size in CHUNKS[1:]]
        across = [shifted(part, "heads", 2, 1) for part in parts]
        beside = shifted(latents, "cfg", 2, 1)
        weight = preload(qkv_weight)
        places = jnp.stack([me, me ^ 1, me ^ 2, me ^ 3]).astype(jnp.int32)
    else:
        gathered = lax.all_gather(latents, ("heads", "cfg"), axis=1, tiled=True)
        weight = qkv_weight
        places = jnp.zeros((1,), jnp.int32)

    def project_chunk(number, before, after):
        start, size = CHUNKS[number]
        if pairs:
            far = ordered(across[number], *before)
            pieces = [latents, beside, far, shifted(far, "cfg", 2, 1)]
            starts = [start, start, 0, 0]
        else:
            pieces, starts = [gathered], [start]
        labels = 0 if number else LABEL_ROWS
        return project(
            places, tile_ids, pieces, after, starts, modulation, weight, query_gain, key_gain, size, labels
        )

    if stacked:
        made = [project_chunk(number, (), ()) for number in range(len(CHUNKS))]
        queries = [(start, query) for (start, size), (query, kv) in zip(CHUNKS, made)]
        spread = [lax.all_gather(kv, "tiles", axis=0) for query, kv in made]
        ids = spread[0][:, CHUNKS[0][1], :per_dev].reshape(-1).astype(jnp.int32)
        pieces = [(array, 0) + chunk + (everyone,) for array, chunk in zip(spread, CHUNKS)]
        tokens = (ids, tile_ids, windows)
        attended = attend(tokens, queries, pieces, everyone, [], start=begin, last=True, stacked=True)
    else:
        near = lambda values: lax.ppermute(values, "tiles", NEAR)
        away = lambda values: lax.ppermute(values, "tiles", AWAY)

        def piece(array, source, number, wanted):
            return (array, source) + CHUNKS[number] + (wanted,)

        query0, kv0 = project_chunk(0, (weight, parts[2]) if pairs else (), ())
        near0, away0 = near(kv0), away(kv0)
        query1, kv1 = project_chunk(1, (kv0,), ())
        both0 = near(ordered(away0, near0, kv1))
        near1, away1 = near(kv1), away(ordered(kv1, away0))
        labels = [array[CHUNKS[0][1], :per_dev].astype(jnp.int32) for array in (near0, away0)]
        early = (jnp.concatenate([tile_ids] + labels), tile_ids, windows)
        queries = [(0, query0), (CHUNKS[1][0], query1)]
        pieces = [piece(kv0, 0, 0, [0]), piece(kv1, 0, 1, [0])]
        pieces += [piece(near0, 1, 0, [0]), piece(away0, 2, 0, [0])]
        state = attend(early, queries, pieces, [0], [], start=begin)
        query2, kv2 = project_chunk(2, (kv1,), (state[1],))
        both1 = near(ordered(away1, near1, both0, kv2))
        near2, away2 = near(kv2), away(ordered(kv2, away1))
        labels.append(both0[CHUNKS[0][1], :per_dev].astype(jnp.int32))
        tokens = (jnp.concatenate([tile_ids] + labels), tile_ids, windows)
        queries.append((CHUNKS[2][0], query2))
        pieces = [piece(kv2, 0, 2, [0, 1]), piece(kv0, 0, 0, [1]), piece(kv1, 0, 1, [1])]
        pieces += [piece(near0, 1, 0, [1]), piece(away0, 2, 0, [1]), piece(both0, 3, 0, [0, 1])]
        pieces += [piece(near1, 1, 1, [0, 1]), piece(away1, 2, 1, [0, 1])]
        state = attend(tokens, queries, pieces, [1], [0], start=begin, state=state)
        both2 = near(ordered(away2, near2, both1, state[1]))
        pieces = [piece(both1, 3, 1, [0, 1]), piece(near2, 1, 2, [0, 1]), piece(away2, 2, 2, [0, 1])]
        state = attend(tokens, queries, pieces, [], [0, 1], state=state)
        attended = attend(tokens, queries, [piece(both2, 3, 2, [0, 1])], [], [0, 1], state=state, last=True)

    if pairs:
        far = shifted(attended, "heads", 2, 1)
        pieces = [attended, shifted(attended, "cfg", 2, 1), far, shifted(far, "cfg", 2, 1)]
    else:
        pieces = [lax.all_gather(attended, ("heads", "cfg"), axis=1, tiled=True)]
    gate = modulation if pairs else lax.dynamic_slice_in_dim(modulation[2:3], me * width, width, 1)
    return merge(places, pieces, proj_weight, latents, gate)


def solution(mesh):
    in_specs = (
        P(("groups", "tiles"), ("heads", "cfg")),
        P("groups", None),
        P(None, ("heads", "cfg")),
        P(),
        P(),
        P("groups", ("heads", "cfg")),
        P("groups"),
        P(("groups", "tiles")),
        P("groups", None),
        P(None, ("heads", "cfg")),
    )
    out_specs = P(("groups", "tiles"), ("heads", "cfg"))
    run = functools.partial(body, mesh.shape["heads"], mesh.shape["cfg"], mesh.shape["tiles"])
    return jax.shard_map(run, mesh=mesh, in_specs=in_specs, out_specs=out_specs, check_vma=False)
```

```python
import functools
import math

import jax
import jax.numpy as jnp
from jax import lax
from jax.experimental import pallas as pl
from jax.experimental.pallas import tpu as pltpu
from jax.sharding import PartitionSpec as P

HD = 128
TILE = 384
TXT = 256
CHUNKS = ((0, 128), (128, 256), (384, 384))
LABEL_ROWS = 16

epsilon = 1e-06
LOG2E = math.log2(math.e)
FACTOR = LOG2E / math.sqrt(HD)

SMEM = pl.BlockSpec(memory_space=pltpu.SMEM)
VMEM = pl.BlockSpec(memory_space=pltpu.VMEM)
HBM = pl.BlockSpec(memory_space=pltpu.HBM)
ANY = pl.BlockSpec(memory_space=pl.ANY)
PROJECT_LIMIT = 24 * 2**20
ATTEND_LIMIT = 16 * 2**20
MERGE_LIMIT = 16 * 2**20
NT = (((1,), (1,)), ((), ()))


def rms_norm(values, gain):
    return values * lax.rsqrt(jnp.mean(values * values, axis=-1, keepdims=True) + epsilon) * gain


def project_kernel(count, after, starts, rows, place_ref, ids_ref, *refs):
    sources = refs[:count]
    refs = refs[:count] + refs[count + after :]
    modulation_ref, query_gain_ref, key_gain_ref, weight_ref = refs[count : count + 4]
    query_ref, kv_ref, pieces_ref, piece_sem = refs[count + 4 :]
    width = sources[0].shape[1]
    features = width * count
    spans = []
    piece_copies = []
    for place, (source, start) in enumerate(zip(sources, starts)):
        first = place_ref[place] * width
        if count > 1:
            first = pl.multiple_of(first, width)
        spans.append(pl.ds(first, width))
        piece_copies.append(
            pltpu.make_async_copy(source.at[start : start + rows, :], pieces_ref.at[place], piece_sem.at[place])
        )
    for copy in piece_copies:
        copy.start()
    total = 0.0
    for place, copy in enumerate(piece_copies):
        copy.wait()
        total = total + jnp.sum(pieces_ref[place].astype(jnp.float32), axis=1, keepdims=True)
    average = total / features
    spread = 0.0
    for place in range(count):
        centred = pieces_ref[place].astype(jnp.float32) - average
        spread = spread + jnp.sum(centred * centred, axis=1, keepdims=True)
    scale = lax.rsqrt(spread / features + epsilon)
    projected = 0.0
    for place, span in enumerate(spans):
        centred = pieces_ref[place].astype(jnp.float32) - average
        modulated = (
            centred * scale * (1.0 + modulation_ref[1:2, span]) + modulation_ref[0:1, span]
        ).astype(jnp.bfloat16)
        projected = projected + jnp.dot(modulated, weight_ref[span, :], preferred_element_type=jnp.float32)
    query_ref[...] = rms_norm(projected[:, :HD], query_gain_ref[...]).astype(jnp.bfloat16)
    kv_ref[:rows, :HD] = rms_norm(projected[:, HD : 2 * HD], key_gain_ref[...]).astype(jnp.bfloat16)
    kv_ref[:rows, HD:] = projected[:, 2 * HD :].astype(jnp.bfloat16)
    labels = kv_ref.shape[0] - rows
    if labels:
        lane = lax.broadcasted_iota(jnp.int32, (labels, 2 * HD), 1)
        label = jnp.full((labels, 2 * HD), ids_ref[0], jnp.int32)
        for slot in range(1, ids_ref.shape[0]):
            label = jnp.where(lane == slot, ids_ref[slot], label)
        kv_ref[rows:, :] = label.astype(jnp.float32).astype(jnp.bfloat16)


def preload_kernel(weight_ref, out_ref, sem):
    copy = pltpu.make_async_copy(weight_ref, out_ref, sem)
    copy.start()
    copy.wait()


def preload(weight):
    return pl.pallas_call(
        preload_kernel,
        out_shape=jax.ShapeDtypeStruct(weight.shape, weight.dtype),
        in_specs=[HBM],
        out_specs=VMEM,
        scratch_shapes=[pltpu.SemaphoreType.DMA],
        compiler_params=pltpu.CompilerParams(vmem_limit_bytes=ATTEND_LIMIT),
        cost_estimate=pl.CostEstimate(flops=0, bytes_accessed=4096, transcendentals=0),
    )(weight)


def project(places, ids, pieces, after, starts, modulation, weight, query_gain, key_gain, rows, labels):
    count = len(pieces)
    width = pieces[0].shape[1]
    return pl.pallas_call(
        functools.partial(project_kernel, count, len(after), starts, rows),
        out_shape=(
            jax.ShapeDtypeStruct((rows, HD), jnp.bfloat16),
            jax.ShapeDtypeStruct((rows + labels, 2 * HD), jnp.bfloat16),
        ),
        in_specs=[SMEM] * 2 + [HBM] * count + [ANY] * len(after) + [VMEM] * 4,
        out_specs=(VMEM, VMEM),
        scratch_shapes=[
            pltpu.VMEM((count, rows, width), jnp.bfloat16),
            pltpu.SemaphoreType.DMA((count,)),
        ],
        compiler_params=pltpu.CompilerParams(vmem_limit_bytes=PROJECT_LIMIT),
        cost_estimate=pl.CostEstimate(flops=rows, bytes_accessed=rows, transcendentals=rows),
    )(places, ids, *pieces, *after, modulation, query_gain, key_gain, weight)


def attend_block(query, shift, keys, values):
    scores = lax.dot_general(query, keys, NT, preferred_element_type=jnp.float32)
    strips = [
        jnp.exp2(scores[:, at : at + HD] * FACTOR - shift) for at in range(0, keys.shape[0], HD)
    ]
    weights = jnp.concatenate(strips, axis=1) if len(strips) > 1 else strips[0]
    product = jnp.dot(weights.astype(jnp.bfloat16), values, preferred_element_type=jnp.float32)
    return sum(strips), product


def segments(start, size):
    out = []
    at = start
    while at < start + size:
        end = min(start + size, (at // TILE + 1) * TILE)
        out.append((at - start, end - at, at // TILE))
        at = end
    return out


def attend_kernel(starts, plan, tiles, begin, held, last, stacked, ids_ref, own_ref, windows_ref, *refs):
    refs = list(refs)
    queries = [refs.pop(0) for _ in starts]
    kvs = [refs.pop(0) for _ in plan]
    if begin:
        length_ref, text_ref, query_gain_ref, key_gain_ref = [refs.pop(0) for _ in range(4)]
    if held:
        shift_in, total_in, accum_in = [refs.pop(0) for _ in range(3)]
    if last:
        out_ref = refs.pop(0)
    shift_ref, total_ref, accum_ref, query_ref = refs
    for start, piece in zip(starts, queries):
        query_ref[start : start + piece.shape[0], :] = piece[...]
    if begin:
        bound = (
            jnp.max(jnp.abs(query_gain_ref[...])) * jnp.max(jnp.abs(key_gain_ref[...])) * (1.02 * HD * FACTOR)
        )
        live = lax.broadcasted_iota(jnp.int32, (TILE, TXT), 1) < length_ref[0]
    for tile in sorted(begin + held):
        rows = slice(tile * TILE, (tile + 1) * TILE)
        if tile in begin:
            scores = lax.dot_general(query_ref[rows, :], text_ref[:, :HD], NT, preferred_element_type=jnp.float32)
            scores = jnp.where(live, scores * FACTOR, -jnp.inf)
            top = jnp.maximum(jnp.max(scores, axis=1, keepdims=True), bound)
            weights = jnp.exp2(scores - top)
            shift_ref[rows, :] = jnp.broadcast_to(top, (TILE, HD))
            total_ref[rows, :] = weights[:, :HD] + weights[:, HD:]
            accum_ref[rows, :] = jnp.dot(
                weights.astype(jnp.bfloat16), text_ref[:, HD:], preferred_element_type=jnp.float32
            )
        else:
            shift_ref[rows, :] = shift_in[rows, :]
            total_ref[rows, :] = total_in[rows, :]
            accum_ref[rows, :] = accum_in[rows, :]
        own = own_ref[tile]
        reach = 0
        for entry in range(windows_ref.shape[1]):
            reach = reach | (1 << windows_ref[own, entry])
        groups = {}
        for number, (source, start, size, wanted) in enumerate(plan):
            if tile in wanted:
                for at, length, slot in segments(start, size):
                    groups.setdefault((source, slot), []).append((number, slice(at, at + length)))
        for (source, slot), blocks in groups.items():

            def work(source, view, rows=rows, reach=reach, slot=slot, blocks=blocks):
                @pl.when(((reach >> ids_ref[source * tiles + slot]) & 1) > 0)
                def _():
                    parts = [
                        attend_block(
                            query_ref[rows, :], shift_ref[rows, :], view(number)[span, :HD], view(number)[span, HD:]
                        )
                        for number, span in blocks
                    ]
                    total_ref[rows, :] += sum(total for total, product in parts)
                    accum_ref[rows, :] += sum(product for total, product in parts)

            if stacked:

                def step(source, carry, work=work):
                    work(source, lambda number: kvs[number].at[source])
                    return carry

                lax.fori_loop(0, kvs[0].shape[0], step, 0)
            else:
                work(source, lambda number: kvs[number])
        if last:
            total = jnp.sum(total_ref[rows, :], axis=1, keepdims=True)
            out_ref[rows, :] = (accum_ref[rows, :] / total).astype(jnp.bfloat16)


def attend(tokens, queries, pieces, begin, held, start=(), state=(), last=False, stacked=False):
    ids, own_ids, windows = tokens
    tiles = own_ids.shape[0]
    rows = tiles * TILE
    part = jax.ShapeDtypeStruct((rows, HD), jnp.float32)
    scratch = [pltpu.VMEM((rows, HD), jnp.bfloat16)]
    if last:
        out_shape = jax.ShapeDtypeStruct((rows, HD), jnp.bfloat16)
        scratch = [pltpu.VMEM((rows, HD), jnp.float32)] * 3 + scratch
    else:
        out_shape = (part,) * 3
    keys = sum(piece[0].size // (2 * HD) for piece in pieces)
    extra = (tuple(start) if begin else ()) + tuple(state)
    return pl.pallas_call(
        functools.partial(
            attend_kernel, [at for at, array in queries], [piece[1:] for piece in pieces], tiles, begin, held, last, stacked
        ),
        out_shape=out_shape,
        in_specs=[SMEM] * 3
        + [VMEM] * (len(queries) + len(pieces))
        + ([SMEM] + [VMEM] * 3 if begin else [])
        + [VMEM] * len(state),
        out_specs=VMEM if last else (VMEM,) * 3,
        scratch_shapes=scratch,
        compiler_params=pltpu.CompilerParams(vmem_limit_bytes=ATTEND_LIMIT),
        cost_estimate=pl.CostEstimate(flops=rows * keys, bytes_accessed=rows * HD, transcendentals=rows),
    )(ids, own_ids, windows, *[array for at, array in queries], *[piece[0] for piece in pieces], *extra)


def merge_kernel(count, block, place_ref, *refs):
    pieces = refs[:count]
    weight_ref, latents_ref, gate_ref, out_ref, joined_ref, made_ref, sem = refs[count:]
    depth = pieces[0].shape[1]
    width = latents_ref.shape[1]
    if count > 1:
        gate = gate_ref[2:3, pl.ds(pl.multiple_of(place_ref[0] * width, width), width)]
        for place, piece in enumerate(pieces):
            joined_ref[:, pl.ds(pl.multiple_of(place_ref[place] * depth, depth), depth)] = piece[...]
    else:
        gate = gate_ref[...]
        joined_ref[...] = pieces[0][...]
    copies = []
    for number in range(latents_ref.shape[0] // block):
        rows = slice(number * block, (number + 1) * block)
        product = jnp.dot(joined_ref[rows, :], weight_ref[...], preferred_element_type=jnp.float32)
        made_ref[rows, :] = (latents_ref[rows, :].astype(jnp.float32) + gate * product).astype(jnp.bfloat16)
        copies.append(pltpu.make_async_copy(made_ref.at[rows, :], out_ref.at[rows, :], sem.at[number]))
        copies[-1].start()
    for copy in copies:
        copy.wait()


def merge(places, pieces, weight, latents, gate):
    rows, width = latents.shape
    block = 256
    return pl.pallas_call(
        functools.partial(merge_kernel, len(pieces), block),
        out_shape=jax.ShapeDtypeStruct((rows, width), jnp.bfloat16),
        in_specs=[SMEM] + [VMEM] * (len(pieces) + 3),
        out_specs=HBM,
        scratch_shapes=[
            pltpu.VMEM((rows, weight.shape[0]), jnp.bfloat16),
            pltpu.VMEM((rows, width), jnp.bfloat16),
            pltpu.SemaphoreType.DMA((rows // block,)),
        ],
        compiler_params=pltpu.CompilerParams(vmem_limit_bytes=MERGE_LIMIT),
        cost_estimate=pl.CostEstimate(
            flops=2 * rows * width * weight.shape[0],
            bytes_accessed=rows * width * 4 + weight.size * 2 + rows * weight.shape[0] * 2,
            transcendentals=0,
        ),
    )(places, *pieces, weight, latents, gate)


def shifted(values, axis, size, by):
    return lax.ppermute(values, axis, [(at, (at + by) % size) for at in range(size)])


LINE = 4


NEAR = [(0, 1), (1, 0), (2, 3), (3, 2)]
AWAY = [(0, 2), (1, 3), (2, 0), (3, 1)]


def ordered(values, *before):
    return lax.optimization_barrier((values, *before))[0]


def body(
    heads_size,
    cfg_size,
    tiles_size,
    latents,
    modulation,
    qkv_weight,
    query_gain,
    key_gain,
    text_kv,
    text_len,
    tile_ids,
    windows,
    proj_weight,
):
    pairs = heads_size == 2 and cfg_size == 2
    stacked = tiles_size != LINE
    per_dev = tile_ids.shape[0]
    width = latents.shape[1]
    me = lax.axis_index(("heads", "cfg"))
    query_gain = query_gain[None, :]
    key_gain = key_gain[None, :]

    begin = (text_len, text_kv, query_gain, key_gain)
    everyone = list(range(per_dev))

    if pairs:
        parts = [latents[: CHUNKS[0][1]]]
        rest = ordered(latents, parts[0])
        parts += [rest[start : start + size] for start, size in CHUNKS[1:]]
        across = [shifted(part, "heads", 2, 1) for part in parts]
        beside = shifted(latents, "cfg", 2, 1)
        weight = preload(qkv_weight)
        places = jnp.stack([me, me ^ 1, me ^ 2, me ^ 3]).astype(jnp.int32)
    else:
        gathered = lax.all_gather(latents, ("heads", "cfg"), axis=1, tiled=True)
        weight = qkv_weight
        places = jnp.zeros((1,), jnp.int32)

    def project_chunk(number, before, after):
        start, size = CHUNKS[number]
        if pairs:
            far = ordered(across[number], *before)
            pieces = [latents, beside, far, shifted(far, "cfg", 2, 1)]
            starts = [start, start, 0, 0]
        else:
            pieces, starts = [gathered], [start]
        labels = 0 if number else LABEL_ROWS
        return project(
            places, tile_ids, pieces, after, starts, modulation, weight, query_gain, key_gain, size, labels
        )

    if stacked:
        made = [project_chunk(number, (), ()) for number in range(len(CHUNKS))]
        queries = [(start, query) for (start, size), (query, kv) in zip(CHUNKS, made)]
        spread = [lax.all_gather(kv, "tiles", axis=0) for query, kv in made]
        ids = spread[0][:, CHUNKS[0][1], :per_dev].reshape(-1).astype(jnp.int32)
        pieces = [(array, 0) + chunk + (everyone,) for array, chunk in zip(spread, CHUNKS)]
        tokens = (ids, tile_ids, windows)
        attended = attend(tokens, queries, pieces, everyone, [], start=begin, last=True, stacked=True)
    else:
        near = lambda values: lax.ppermute(values, "tiles", NEAR)
        away = lambda values: lax.ppermute(values, "tiles", AWAY)

        def piece(array, source, number, wanted):
            return (array, source) + CHUNKS[number] + (wanted,)

        query0, kv0 = project_chunk(0, (weight, parts[2]) if pairs else (), ())
        near0, away0 = near(kv0), away(kv0)
        query1, kv1 = project_chunk(1, (kv0,), ())
        both0 = near(ordered(away0, near0, kv1))
        near1, away1 = near(kv1), away(ordered(kv1, away0))
        labels = [array[CHUNKS[0][1], :per_dev].astype(jnp.int32) for array in (near0, away0)]
        early = (jnp.concatenate([tile_ids] + labels), tile_ids, windows)
        queries = [(0, query0), (CHUNKS[1][0], query1)]
        pieces = [piece(kv0, 0, 0, [0]), piece(kv1, 0, 1, [0])]
        state = attend((tile_ids, tile_ids, windows), queries, pieces, [0], [], start=begin)
        query2, kv2 = project_chunk(2, (kv1, state[1], near0, away0), ())
        both1 = near(ordered(away1, near1, both0, kv2))
        near2, away2 = near(kv2), away(ordered(kv2, away1))
        labels.append(both0[CHUNKS[0][1], :per_dev].astype(jnp.int32))
        tokens = (jnp.concatenate([tile_ids] + labels), tile_ids, windows)
        queries.append((CHUNKS[2][0], query2))
        pieces = [piece(kv2, 0, 2, [0, 1]), piece(kv0, 0, 0, [1]), piece(kv1, 0, 1, [1])]
        pieces += [piece(near0, 1, 0, [0, 1]), piece(away0, 2, 0, [0, 1]), piece(both0, 3, 0, [0, 1])]
        pieces += [piece(near1, 1, 1, [0, 1]), piece(away1, 2, 1, [0, 1])]
        state = attend(tokens, queries, pieces, [1], [0], start=begin, state=state)
        both2 = near(ordered(away2, near2, both1, state[1]))
        pieces = [piece(both1, 3, 1, [0, 1]), piece(near2, 1, 2, [0, 1]), piece(away2, 2, 2, [0, 1])]
        state = attend(tokens, queries, pieces, [], [0, 1], state=state)
        attended = attend(tokens, queries, [piece(both2, 3, 2, [0, 1])], [], [0, 1], state=state, last=True)

    if pairs:
        far = shifted(attended, "heads", 2, 1)
        pieces = [attended, shifted(attended, "cfg", 2, 1), far, shifted(far, "cfg", 2, 1)]
    else:
        pieces = [lax.all_gather(attended, ("heads", "cfg"), axis=1, tiled=True)]
    gate = modulation if pairs else lax.dynamic_slice_in_dim(modulation[2:3], me * width, width, 1)
    return merge(places, pieces, proj_weight, latents, gate)


def solution(mesh):
    in_specs = (
        P(("groups", "tiles"), ("heads", "cfg")),
        P("groups", None),
        P(None, ("heads", "cfg")),
        P(),
        P(),
        P("groups", ("heads", "cfg")),
        P("groups"),
        P(("groups", "tiles")),
        P("groups", None),
        P(None, ("heads", "cfg")),
    )
    out_specs = P(("groups", "tiles"), ("heads", "cfg"))
    run = functools.partial(body, mesh.shape["heads"], mesh.shape["cfg"], mesh.shape["tiles"])
    return jax.shard_map(run, mesh=mesh, in_specs=in_specs, out_specs=out_specs, check_vma=False)
```

```python
import functools
import math

import jax
import jax.numpy as jnp
from jax import lax
from jax.experimental import pallas as pl
from jax.experimental.pallas import tpu as pltpu
from jax.sharding import PartitionSpec as P

HD = 128
TILE = 384
TXT = 256
CHUNKS = ((0, 128), (128, 256), (384, 384))
LABEL_ROWS = 16

epsilon = 1e-06
LOG2E = math.log2(math.e)
FACTOR = LOG2E / math.sqrt(HD)

SMEM = pl.BlockSpec(memory_space=pltpu.SMEM)
VMEM = pl.BlockSpec(memory_space=pltpu.VMEM)
HBM = pl.BlockSpec(memory_space=pltpu.HBM)
ANY = pl.BlockSpec(memory_space=pl.ANY)
PROJECT_LIMIT = 24 * 2**20
ATTEND_LIMIT = 16 * 2**20
MERGE_LIMIT = 16 * 2**20
NT = (((1,), (1,)), ((), ()))


def rms_norm(values, gain):
    return values * lax.rsqrt(jnp.mean(values * values, axis=-1, keepdims=True) + epsilon) * gain


def project_kernel(count, after, starts, rows, place_ref, ids_ref, *refs):
    sources = refs[:count]
    refs = refs[:count] + refs[count + after :]
    modulation_ref, query_gain_ref, key_gain_ref, weight_ref = refs[count : count + 4]
    query_ref, kv_ref = refs[count + 4 :]
    width = sources[0].shape[1]
    features = width * count
    spans = []
    pieces = []
    for place, (source, start) in enumerate(zip(sources, starts)):
        first = place_ref[place] * width
        if count > 1:
            first = pl.multiple_of(first, width)
        spans.append(pl.ds(first, width))
        pieces.append(source.at[start : start + rows, :])
    total = 0.0
    for piece in pieces:
        total = total + jnp.sum(piece[...].astype(jnp.float32), axis=1, keepdims=True)
    average = total / features
    spread = 0.0
    for place in range(count):
        centred = pieces[place][...].astype(jnp.float32) - average
        spread = spread + jnp.sum(centred * centred, axis=1, keepdims=True)
    scale = lax.rsqrt(spread / features + epsilon)
    projected = 0.0
    for place, span in enumerate(spans):
        centred = pieces[place][...].astype(jnp.float32) - average
        modulated = (
            centred * scale * (1.0 + modulation_ref[1:2, span]) + modulation_ref[0:1, span]
        ).astype(jnp.bfloat16)
        projected = projected + jnp.dot(modulated, weight_ref[span, :], preferred_element_type=jnp.float32)
    query_ref[...] = rms_norm(projected[:, :HD], query_gain_ref[...]).astype(jnp.bfloat16)
    kv_ref[:rows, :HD] = rms_norm(projected[:, HD : 2 * HD], key_gain_ref[...]).astype(jnp.bfloat16)
    kv_ref[:rows, HD:] = projected[:, 2 * HD :].astype(jnp.bfloat16)
    labels = kv_ref.shape[0] - rows
    if labels:
        lane = lax.broadcasted_iota(jnp.int32, (labels, 2 * HD), 1)
        label = jnp.full((labels, 2 * HD), ids_ref[0], jnp.int32)
        for slot in range(1, ids_ref.shape[0]):
            label = jnp.where(lane == slot, ids_ref[slot], label)
        kv_ref[rows:, :] = label.astype(jnp.float32).astype(jnp.bfloat16)


def preload_kernel(weight_ref, out_ref, sem):
    copy = pltpu.make_async_copy(weight_ref, out_ref, sem)
    copy.start()
    copy.wait()


def preload(weight):
    return pl.pallas_call(
        preload_kernel,
        out_shape=jax.ShapeDtypeStruct(weight.shape, weight.dtype),
        in_specs=[HBM],
        out_specs=VMEM,
        scratch_shapes=[pltpu.SemaphoreType.DMA],
        compiler_params=pltpu.CompilerParams(vmem_limit_bytes=ATTEND_LIMIT),
        cost_estimate=pl.CostEstimate(flops=0, bytes_accessed=4096, transcendentals=0),
    )(weight)


def project(places, ids, pieces, after, starts, modulation, weight, query_gain, key_gain, rows, labels):
    count = len(pieces)
    width = pieces[0].shape[1]
    return pl.pallas_call(
        functools.partial(project_kernel, count, len(after), starts, rows),
        out_shape=(
            jax.ShapeDtypeStruct((rows, HD), jnp.bfloat16),
            jax.ShapeDtypeStruct((rows + labels, 2 * HD), jnp.bfloat16),
        ),
        in_specs=[SMEM] * 2 + [VMEM] * count + [ANY] * len(after) + [VMEM] * 4,
        out_specs=(VMEM, VMEM),
        compiler_params=pltpu.CompilerParams(vmem_limit_bytes=PROJECT_LIMIT),
        cost_estimate=pl.CostEstimate(flops=rows, bytes_accessed=rows, transcendentals=rows),
    )(places, ids, *pieces, *after, modulation, query_gain, key_gain, weight)


def attend_block(query, shift, keys, values):
    scores = lax.dot_general(query, keys, NT, preferred_element_type=jnp.float32)
    strips = [
        jnp.exp2(scores[:, at : at + HD] * FACTOR - shift) for at in range(0, keys.shape[0], HD)
    ]
    weights = jnp.concatenate(strips, axis=1) if len(strips) > 1 else strips[0]
    product = jnp.dot(weights.astype(jnp.bfloat16), values, preferred_element_type=jnp.float32)
    return sum(strips), product


def segments(start, size):
    out = []
    at = start
    while at < start + size:
        end = min(start + size, (at // TILE + 1) * TILE)
        out.append((at - start, end - at, at // TILE))
        at = end
    return out


def attend_kernel(starts, plan, tiles, begin, held, last, stacked, ids_ref, own_ref, windows_ref, *refs):
    refs = list(refs)
    queries = [refs.pop(0) for _ in starts]
    kvs = [refs.pop(0) for _ in plan]
    if begin:
        length_ref, text_ref, query_gain_ref, key_gain_ref = [refs.pop(0) for _ in range(4)]
    if held:
        shift_in, total_in, accum_in = [refs.pop(0) for _ in range(3)]
    if last:
        out_ref = refs.pop(0)
    shift_ref, total_ref, accum_ref, query_ref = refs
    for start, piece in zip(starts, queries):
        query_ref[start : start + piece.shape[0], :] = piece[...]
    if begin:
        bound = (
            jnp.max(jnp.abs(query_gain_ref[...])) * jnp.max(jnp.abs(key_gain_ref[...])) * (1.02 * HD * FACTOR)
        )
        live = lax.broadcasted_iota(jnp.int32, (TILE, TXT), 1) < length_ref[0]
    for tile in sorted(begin + held):
        rows = slice(tile * TILE, (tile + 1) * TILE)
        if tile in begin:
            scores = lax.dot_general(query_ref[rows, :], text_ref[:, :HD], NT, preferred_element_type=jnp.float32)
            scores = jnp.where(live, scores * FACTOR, -jnp.inf)
            top = jnp.maximum(jnp.max(scores, axis=1, keepdims=True), bound)
            weights = jnp.exp2(scores - top)
            shift_ref[rows, :] = jnp.broadcast_to(top, (TILE, HD))
            total_ref[rows, :] = weights[:, :HD] + weights[:, HD:]
            accum_ref[rows, :] = jnp.dot(
                weights.astype(jnp.bfloat16), text_ref[:, HD:], preferred_element_type=jnp.float32
            )
        else:
            shift_ref[rows, :] = shift_in[rows, :]
            total_ref[rows, :] = total_in[rows, :]
            accum_ref[rows, :] = accum_in[rows, :]
        own = own_ref[tile]
        reach = 0
        for entry in range(windows_ref.shape[1]):
            reach = reach | (1 << windows_ref[own, entry])
        groups = {}
        for number, (source, start, size, wanted) in enumerate(plan):
            if tile in wanted:
                for at, length, slot in segments(start, size):
                    groups.setdefault((source, slot), []).append((number, slice(at, at + length)))
        for (source, slot), blocks in groups.items():

            def work(source, view, rows=rows, reach=reach, slot=slot, blocks=blocks):
                @pl.when(((reach >> ids_ref[source * tiles + slot]) & 1) > 0)
                def _():
                    parts = [
                        attend_block(
                            query_ref[rows, :], shift_ref[rows, :], view(number)[span, :HD], view(number)[span, HD:]
                        )
                        for number, span in blocks
                    ]
                    total_ref[rows, :] += sum(total for total, product in parts)
                    accum_ref[rows, :] += sum(product for total, product in parts)

            if stacked:

                def step(source, carry, work=work):
                    work(source, lambda number: kvs[number].at[source])
                    return carry

                lax.fori_loop(0, kvs[0].shape[0], step, 0)
            else:
                work(source, lambda number: kvs[number])
        if last:
            total = jnp.sum(total_ref[rows, :], axis=1, keepdims=True)
            out_ref[rows, :] = (accum_ref[rows, :] / total).astype(jnp.bfloat16)


def attend(tokens, queries, pieces, begin, held, start=(), state=(), last=False, stacked=False):
    ids, own_ids, windows = tokens
    tiles = own_ids.shape[0]
    rows = tiles * TILE
    part = jax.ShapeDtypeStruct((rows, HD), jnp.float32)
    scratch = [pltpu.VMEM((rows, HD), jnp.bfloat16)]
    if last:
        out_shape = jax.ShapeDtypeStruct((rows, HD), jnp.bfloat16)
        scratch = [pltpu.VMEM((rows, HD), jnp.float32)] * 3 + scratch
    else:
        out_shape = (part,) * 3
    keys = sum(piece[0].size // (2 * HD) for piece in pieces)
    extra = (tuple(start) if begin else ()) + tuple(state)
    return pl.pallas_call(
        functools.partial(
            attend_kernel, [at for at, array in queries], [piece[1:] for piece in pieces], tiles, begin, held, last, stacked
        ),
        out_shape=out_shape,
        in_specs=[SMEM] * 3
        + [VMEM] * (len(queries) + len(pieces))
        + ([SMEM] + [VMEM] * 3 if begin else [])
        + [VMEM] * len(state),
        out_specs=VMEM if last else (VMEM,) * 3,
        scratch_shapes=scratch,
        compiler_params=pltpu.CompilerParams(vmem_limit_bytes=ATTEND_LIMIT),
        cost_estimate=pl.CostEstimate(flops=rows * keys, bytes_accessed=rows * HD, transcendentals=rows),
    )(ids, own_ids, windows, *[array for at, array in queries], *[piece[0] for piece in pieces], *extra)


def merge_kernel(count, block, place_ref, *refs):
    pieces = refs[:count]
    weight_ref, latents_ref, gate_ref, out_ref, joined_ref, made_ref, sem = refs[count:]
    depth = pieces[0].shape[1]
    width = latents_ref.shape[1]
    if count > 1:
        gate = gate_ref[2:3, pl.ds(pl.multiple_of(place_ref[0] * width, width), width)]
        for place, piece in enumerate(pieces):
            joined_ref[:, pl.ds(pl.multiple_of(place_ref[place] * depth, depth), depth)] = piece[...]
    else:
        gate = gate_ref[...]
        joined_ref[...] = pieces[0][...]
    copies = []
    for number in range(latents_ref.shape[0] // block):
        rows = slice(number * block, (number + 1) * block)
        product = jnp.dot(joined_ref[rows, :], weight_ref[...], preferred_element_type=jnp.float32)
        made_ref[rows, :] = (latents_ref[rows, :].astype(jnp.float32) + gate * product).astype(jnp.bfloat16)
        copies.append(pltpu.make_async_copy(made_ref.at[rows, :], out_ref.at[rows, :], sem.at[number]))
        copies[-1].start()
    for copy in copies:
        copy.wait()


def merge(places, pieces, weight, latents, gate):
    rows, width = latents.shape
    block = 256
    return pl.pallas_call(
        functools.partial(merge_kernel, len(pieces), block),
        out_shape=jax.ShapeDtypeStruct((rows, width), jnp.bfloat16),
        in_specs=[SMEM] + [VMEM] * (len(pieces) + 3),
        out_specs=HBM,
        scratch_shapes=[
            pltpu.VMEM((rows, weight.shape[0]), jnp.bfloat16),
            pltpu.VMEM((rows, width), jnp.bfloat16),
            pltpu.SemaphoreType.DMA((rows // block,)),
        ],
        compiler_params=pltpu.CompilerParams(vmem_limit_bytes=MERGE_LIMIT),
        cost_estimate=pl.CostEstimate(
            flops=2 * rows * width * weight.shape[0],
            bytes_accessed=rows * width * 4 + weight.size * 2 + rows * weight.shape[0] * 2,
            transcendentals=0,
        ),
    )(places, *pieces, weight, latents, gate)


def shifted(values, axis, size, by):
    return lax.ppermute(values, axis, [(at, (at + by) % size) for at in range(size)])


LINE = 4


NEAR = [(0, 1), (1, 0), (2, 3), (3, 2)]
AWAY = [(0, 2), (1, 3), (2, 0), (3, 1)]


def ordered(values, *before):
    return lax.optimization_barrier((values, *before))[0]


def body(
    heads_size,
    cfg_size,
    tiles_size,
    latents,
    modulation,
    qkv_weight,
    query_gain,
    key_gain,
    text_kv,
    text_len,
    tile_ids,
    windows,
    proj_weight,
):
    pairs = heads_size == 2 and cfg_size == 2
    stacked = tiles_size != LINE
    per_dev = tile_ids.shape[0]
    width = latents.shape[1]
    me = lax.axis_index(("heads", "cfg"))
    query_gain = query_gain[None, :]
    key_gain = key_gain[None, :]

    begin = (text_len, text_kv, query_gain, key_gain)
    everyone = list(range(per_dev))

    if pairs:
        parts = [latents[: CHUNKS[0][1]]]
        rest = ordered(latents, parts[0])
        parts += [rest[start : start + size] for start, size in CHUNKS[1:]]
        across = [shifted(part, "heads", 2, 1) for part in parts]
        beside = shifted(latents, "cfg", 2, 1)
        weight = preload(qkv_weight)
        places = jnp.stack([me, me ^ 1, me ^ 2, me ^ 3]).astype(jnp.int32)
    else:
        gathered = lax.all_gather(latents, ("heads", "cfg"), axis=1, tiled=True)
        weight = qkv_weight
        places = jnp.zeros((1,), jnp.int32)

    def project_chunk(number, before, after):
        start, size = CHUNKS[number]
        if pairs:
            far = ordered(across[number], *before)
            pieces = [latents, beside, far, shifted(far, "cfg", 2, 1)]
            starts = [start, start, 0, 0]
        else:
            pieces, starts = [gathered], [start]
        labels = 0 if number else LABEL_ROWS
        return project(
            places, tile_ids, pieces, after, starts, modulation, weight, query_gain, key_gain, size, labels
        )

    if stacked:
        made = [project_chunk(number, (), ()) for number in range(len(CHUNKS))]
        queries = [(start, query) for (start, size), (query, kv) in zip(CHUNKS, made)]
        spread = [lax.all_gather(kv, "tiles", axis=0) for query, kv in made]
        ids = spread[0][:, CHUNKS[0][1], :per_dev].reshape(-1).astype(jnp.int32)
        pieces = [(array, 0) + chunk + (everyone,) for array, chunk in zip(spread, CHUNKS)]
        tokens = (ids, tile_ids, windows)
        attended = attend(tokens, queries, pieces, everyone, [], start=begin, last=True, stacked=True)
    else:
        near = lambda values: lax.ppermute(values, "tiles", NEAR)
        away = lambda values: lax.ppermute(values, "tiles", AWAY)

        def piece(array, source, number, wanted):
            return (array, source) + CHUNKS[number] + (wanted,)

        query0, kv0 = project_chunk(0, (weight, parts[2]) if pairs else (), ())
        near0, away0 = near(kv0), away(kv0)
        query1, kv1 = project_chunk(1, (kv0,), ())
        both0 = near(ordered(away0, near0, kv1))
        near1, away1 = near(kv1), away(ordered(kv1, away0))
        labels = [array[CHUNKS[0][1], :per_dev].astype(jnp.int32) for array in (near0, away0)]
        early = (jnp.concatenate([tile_ids] + labels), tile_ids, windows)
        queries = [(0, query0), (CHUNKS[1][0], query1)]
        pieces = [piece(kv0, 0, 0, [0]), piece(kv1, 0, 1, [0])]
        state = attend((tile_ids, tile_ids, windows), queries, pieces, [0], [], start=begin)
        query2, kv2 = project_chunk(2, (kv1, state[1], near0, away0), ())
        both1 = near(ordered(away1, near1, both0, kv2))
        near2, away2 = near(kv2), away(ordered(kv2, away1))
        labels.append(both0[CHUNKS[0][1], :per_dev].astype(jnp.int32))
        tokens = (jnp.concatenate([tile_ids] + labels), tile_ids, windows)
        queries.append((CHUNKS[2][0], query2))
        pieces = [piece(kv2, 0, 2, [0, 1]), piece(kv0, 0, 0, [1]), piece(kv1, 0, 1, [1])]
        pieces += [piece(near0, 1, 0, [0, 1]), piece(away0, 2, 0, [0, 1]), piece(both0, 3, 0, [0, 1])]
        pieces += [piece(near1, 1, 1, [0, 1]), piece(away1, 2, 1, [0, 1])]
        state = attend(tokens, queries, pieces, [1], [0], start=begin, state=state)
        both2 = near(ordered(away2, near2, both1, state[1]))
        pieces = [piece(both1, 3, 1, [0, 1]), piece(near2, 1, 2, [0, 1]), piece(away2, 2, 2, [0, 1])]
        state = attend(tokens, queries, pieces, [], [0, 1], state=state)
        attended = attend(tokens, queries, [piece(both2, 3, 2, [0, 1])], [], [0, 1], state=state, last=True)

    if pairs:
        far = shifted(attended, "heads", 2, 1)
        pieces = [attended, shifted(attended, "cfg", 2, 1), far, shifted(far, "cfg", 2, 1)]
    else:
        pieces = [lax.all_gather(attended, ("heads", "cfg"), axis=1, tiled=True)]
    gate = modulation if pairs else lax.dynamic_slice_in_dim(modulation[2:3], me * width, width, 1)
    return merge(places, pieces, proj_weight, latents, gate)


def solution(mesh):
    in_specs = (
        P(("groups", "tiles"), ("heads", "cfg")),
        P("groups", None),
        P(None, ("heads", "cfg")),
        P(),
        P(),
        P("groups", ("heads", "cfg")),
        P("groups"),
        P(("groups", "tiles")),
        P("groups", None),
        P(None, ("heads", "cfg")),
    )
    out_specs = P(("groups", "tiles"), ("heads", "cfg"))
    run = functools.partial(body, mesh.shape["heads"], mesh.shape["cfg"], mesh.shape["tiles"])
    return jax.shard_map(run, mesh=mesh, in_specs=in_specs, out_specs=out_specs, check_vma=False)
```

```python
import functools
import math

import jax
import jax.numpy as jnp
from jax import lax
from jax.experimental import pallas as pl
from jax.experimental.pallas import tpu as pltpu
from jax.sharding import PartitionSpec as P

HD = 128
TILE = 384
TXT = 256
CHUNKS = ((0, 128), (128, 256), (384, 384))
LABEL_ROWS = 16

epsilon = 1e-06
LOG2E = math.log2(math.e)
FACTOR = LOG2E / math.sqrt(HD)

SMEM = pl.BlockSpec(memory_space=pltpu.SMEM)
VMEM = pl.BlockSpec(memory_space=pltpu.VMEM)
HBM = pl.BlockSpec(memory_space=pltpu.HBM)
ANY = pl.BlockSpec(memory_space=pl.ANY)
PROJECT_LIMIT = 24 * 2**20
ATTEND_LIMIT = 16 * 2**20
MERGE_LIMIT = 16 * 2**20
NT = (((1,), (1,)), ((), ()))


def rms_norm(values, gain):
    return values * lax.rsqrt(jnp.mean(values * values, axis=-1, keepdims=True) + epsilon) * gain


def project_kernel(count, after, starts, rows, place_ref, ids_ref, *refs):
    sources = refs[:count]
    refs = refs[:count] + refs[count + after :]
    modulation_ref, query_gain_ref, key_gain_ref, weight_ref = refs[count : count + 4]
    query_ref, kv_ref = refs[count + 4 :]
    width = sources[0].shape[1]
    features = width * count
    spans = []
    pieces = []
    for place, (source, start) in enumerate(zip(sources, starts)):
        first = place_ref[place] * width
        if count > 1:
            first = pl.multiple_of(first, width)
        spans.append(pl.ds(first, width))
        pieces.append(source.at[start : start + rows, :])
    total = 0.0
    for piece in pieces:
        total = total + jnp.sum(piece[...].astype(jnp.float32), axis=1, keepdims=True)
    average = total / features
    spread = 0.0
    for place in range(count):
        centred = pieces[place][...].astype(jnp.float32) - average
        spread = spread + jnp.sum(centred * centred, axis=1, keepdims=True)
    scale = lax.rsqrt(spread / features + epsilon)
    projected = 0.0
    for place, span in enumerate(spans):
        centred = pieces[place][...].astype(jnp.float32) - average
        modulated = (
            centred * scale * (1.0 + modulation_ref[1:2, span]) + modulation_ref[0:1, span]
        ).astype(jnp.bfloat16)
        projected = projected + jnp.dot(modulated, weight_ref[span, :], preferred_element_type=jnp.float32)
    query_ref[...] = rms_norm(projected[:, :HD], query_gain_ref[...]).astype(jnp.bfloat16)
    kv_ref[:rows, :HD] = rms_norm(projected[:, HD : 2 * HD], key_gain_ref[...]).astype(jnp.bfloat16)
    kv_ref[:rows, HD:] = projected[:, 2 * HD :].astype(jnp.bfloat16)
    labels = kv_ref.shape[0] - rows
    if labels:
        lane = lax.broadcasted_iota(jnp.int32, (labels, 2 * HD), 1)
        label = jnp.full((labels, 2 * HD), ids_ref[0], jnp.int32)
        for slot in range(1, ids_ref.shape[0]):
            label = jnp.where(lane == slot, ids_ref[slot], label)
        kv_ref[rows:, :] = label.astype(jnp.float32).astype(jnp.bfloat16)


def preload_kernel(weight_ref, out_ref, sem):
    copy = pltpu.make_async_copy(weight_ref, out_ref, sem)
    copy.start()
    copy.wait()


def preload(weight):
    return pl.pallas_call(
        preload_kernel,
        out_shape=jax.ShapeDtypeStruct(weight.shape, weight.dtype),
        in_specs=[HBM],
        out_specs=VMEM,
        scratch_shapes=[pltpu.SemaphoreType.DMA],
        compiler_params=pltpu.CompilerParams(vmem_limit_bytes=ATTEND_LIMIT),
        cost_estimate=pl.CostEstimate(flops=0, bytes_accessed=4096, transcendentals=0),
    )(weight)


def project(places, ids, pieces, after, starts, modulation, weight, query_gain, key_gain, rows, labels):
    count = len(pieces)
    width = pieces[0].shape[1]
    return pl.pallas_call(
        functools.partial(project_kernel, count, len(after), starts, rows),
        out_shape=(
            jax.ShapeDtypeStruct((rows, HD), jnp.bfloat16),
            jax.ShapeDtypeStruct((rows + labels, 2 * HD), jnp.bfloat16),
        ),
        in_specs=[SMEM] * 2 + [VMEM] * count + [ANY] * len(after) + [VMEM] * 4,
        out_specs=(VMEM, VMEM),
        compiler_params=pltpu.CompilerParams(vmem_limit_bytes=PROJECT_LIMIT),
        cost_estimate=pl.CostEstimate(flops=rows, bytes_accessed=rows, transcendentals=rows),
    )(places, ids, *pieces, *after, modulation, query_gain, key_gain, weight)


def attend_block(query, shift, keys, values):
    scores = lax.dot_general(query, keys, NT, preferred_element_type=jnp.float32)
    strips = [
        jnp.exp2(scores[:, at : at + HD] * FACTOR - shift) for at in range(0, keys.shape[0], HD)
    ]
    weights = jnp.concatenate(strips, axis=1) if len(strips) > 1 else strips[0]
    product = jnp.dot(weights.astype(jnp.bfloat16), values, preferred_element_type=jnp.float32)
    return sum(strips), product


def segments(start, size):
    out = []
    at = start
    while at < start + size:
        end = min(start + size, (at // TILE + 1) * TILE)
        out.append((at - start, end - at, at // TILE))
        at = end
    return out


def attend_kernel(starts, plan, tiles, begin, held, last, stacked, ids_ref, own_ref, windows_ref, *refs):
    refs = list(refs)
    queries = [refs.pop(0) for _ in starts]
    kvs = [refs.pop(0) for _ in plan]
    if begin:
        length_ref, text_ref, query_gain_ref, key_gain_ref = [refs.pop(0) for _ in range(4)]
    if held:
        shift_in, total_in, accum_in = [refs.pop(0) for _ in range(3)]
    if last:
        out_ref = refs.pop(0)
    shift_ref, total_ref, accum_ref, query_ref = refs
    kept = last and not begin
    shifts_ref = shift_in if kept else shift_ref
    for start, piece in zip(starts, queries):
        query_ref[start : start + piece.shape[0], :] = piece[...]
    if begin:
        bound = (
            jnp.max(jnp.abs(query_gain_ref[...])) * jnp.max(jnp.abs(key_gain_ref[...])) * (1.02 * HD * FACTOR)
        )
        live = lax.broadcasted_iota(jnp.int32, (TILE, TXT), 1) < length_ref[0]
    for tile in sorted(begin + held):
        rows = slice(tile * TILE, (tile + 1) * TILE)
        if tile in begin:
            scores = lax.dot_general(query_ref[rows, :], text_ref[:, :HD], NT, preferred_element_type=jnp.float32)
            scores = jnp.where(live, scores * FACTOR, -jnp.inf)
            top = jnp.maximum(jnp.max(scores, axis=1, keepdims=True), bound)
            weights = jnp.exp2(scores - top)
            shift_ref[rows, :] = jnp.broadcast_to(top, (TILE, HD))
            total_ref[rows, :] = weights[:, :HD] + weights[:, HD:]
            accum_ref[rows, :] = jnp.dot(
                weights.astype(jnp.bfloat16), text_ref[:, HD:], preferred_element_type=jnp.float32
            )
        else:
            if not kept:
                shift_ref[rows, :] = shift_in[rows, :]
            total_ref[rows, :] = total_in[rows, :]
            accum_ref[rows, :] = accum_in[rows, :]
        own = own_ref[tile]
        reach = 0
        for entry in range(windows_ref.shape[1]):
            reach = reach | (1 << windows_ref[own, entry])
        groups = {}
        for number, (source, start, size, wanted) in enumerate(plan):
            if tile in wanted:
                for at, length, slot in segments(start, size):
                    groups.setdefault((source, slot), []).append((number, slice(at, at + length)))
        for (source, slot), blocks in groups.items():

            def work(source, view, rows=rows, reach=reach, slot=slot, blocks=blocks):
                @pl.when(((reach >> ids_ref[source * tiles + slot]) & 1) > 0)
                def _():
                    parts = [
                        attend_block(
                            query_ref[rows, :], shifts_ref[rows, :], view(number)[span, :HD], view(number)[span, HD:]
                        )
                        for number, span in blocks
                    ]
                    total_ref[rows, :] += sum(total for total, product in parts)
                    accum_ref[rows, :] += sum(product for total, product in parts)

            if stacked:

                def step(source, carry, work=work):
                    work(source, lambda number: kvs[number].at[source])
                    return carry

                lax.fori_loop(0, kvs[0].shape[0], step, 0)
            else:
                work(source, lambda number: kvs[number])
        if last:
            total = jnp.sum(total_ref[rows, :], axis=1, keepdims=True)
            out_ref[rows, :] = (accum_ref[rows, :] / total).astype(jnp.bfloat16)


def attend(tokens, queries, pieces, begin, held, start=(), state=(), last=False, stacked=False):
    ids, own_ids, windows = tokens
    tiles = own_ids.shape[0]
    rows = tiles * TILE
    part = jax.ShapeDtypeStruct((rows, HD), jnp.float32)
    scratch = [pltpu.VMEM((rows, HD), jnp.bfloat16)]
    if last:
        out_shape = jax.ShapeDtypeStruct((rows, HD), jnp.bfloat16)
        scratch = [pltpu.VMEM((rows, HD), jnp.float32)] * 3 + scratch
    else:
        out_shape = (part,) * 3
    keys = sum(piece[0].size // (2 * HD) for piece in pieces)
    extra = (tuple(start) if begin else ()) + tuple(state)
    return pl.pallas_call(
        functools.partial(
            attend_kernel, [at for at, array in queries], [piece[1:] for piece in pieces], tiles, begin, held, last, stacked
        ),
        out_shape=out_shape,
        in_specs=[SMEM] * 3
        + [VMEM] * (len(queries) + len(pieces))
        + ([SMEM] + [VMEM] * 3 if begin else [])
        + [VMEM] * len(state),
        out_specs=VMEM if last else (VMEM,) * 3,
        scratch_shapes=scratch,
        compiler_params=pltpu.CompilerParams(vmem_limit_bytes=ATTEND_LIMIT),
        cost_estimate=pl.CostEstimate(flops=rows * keys, bytes_accessed=rows * HD, transcendentals=rows),
    )(ids, own_ids, windows, *[array for at, array in queries], *[piece[0] for piece in pieces], *extra)


def merge_kernel(count, block, place_ref, *refs):
    pieces = refs[:count]
    weight_ref, latents_ref, gate_ref, out_ref, joined_ref, made_ref, sem = refs[count:]
    depth = pieces[0].shape[1]
    width = latents_ref.shape[1]
    if count > 1:
        gate = gate_ref[2:3, pl.ds(pl.multiple_of(place_ref[0] * width, width), width)]
        for place, piece in enumerate(pieces):
            joined_ref[:, pl.ds(pl.multiple_of(place_ref[place] * depth, depth), depth)] = piece[...]
    else:
        gate = gate_ref[...]
        joined_ref[...] = pieces[0][...]
    copies = []
    for number in range(latents_ref.shape[0] // block):
        rows = slice(number * block, (number + 1) * block)
        product = jnp.dot(joined_ref[rows, :], weight_ref[...], preferred_element_type=jnp.float32)
        made_ref[rows, :] = (latents_ref[rows, :].astype(jnp.float32) + gate * product).astype(jnp.bfloat16)
        copies.append(pltpu.make_async_copy(made_ref.at[rows, :], out_ref.at[rows, :], sem.at[number]))
        copies[-1].start()
    for copy in copies:
        copy.wait()


def merge(places, pieces, weight, latents, gate):
    rows, width = latents.shape
    block = 256
    return pl.pallas_call(
        functools.partial(merge_kernel, len(pieces), block),
        out_shape=jax.ShapeDtypeStruct((rows, width), jnp.bfloat16),
        in_specs=[SMEM] + [VMEM] * (len(pieces) + 3),
        out_specs=HBM,
        scratch_shapes=[
            pltpu.VMEM((rows, weight.shape[0]), jnp.bfloat16),
            pltpu.VMEM((rows, width), jnp.bfloat16),
            pltpu.SemaphoreType.DMA((rows // block,)),
        ],
        compiler_params=pltpu.CompilerParams(vmem_limit_bytes=MERGE_LIMIT),
        cost_estimate=pl.CostEstimate(
            flops=2 * rows * width * weight.shape[0],
            bytes_accessed=rows * width * 4 + weight.size * 2 + rows * weight.shape[0] * 2,
            transcendentals=0,
        ),
    )(places, *pieces, weight, latents, gate)


def shifted(values, axis, size, by):
    return lax.ppermute(values, axis, [(at, (at + by) % size) for at in range(size)])


LINE = 4


NEAR = [(0, 1), (1, 0), (2, 3), (3, 2)]
AWAY = [(0, 2), (1, 3), (2, 0), (3, 1)]


def ordered(values, *before):
    return lax.optimization_barrier((values, *before))[0]


def body(
    heads_size,
    cfg_size,
    tiles_size,
    latents,
    modulation,
    qkv_weight,
    query_gain,
    key_gain,
    text_kv,
    text_len,
    tile_ids,
    windows,
    proj_weight,
):
    pairs = heads_size == 2 and cfg_size == 2
    stacked = tiles_size != LINE
    per_dev = tile_ids.shape[0]
    width = latents.shape[1]
    me = lax.axis_index(("heads", "cfg"))
    query_gain = query_gain[None, :]
    key_gain = key_gain[None, :]

    begin = (text_len, text_kv, query_gain, key_gain)
    everyone = list(range(per_dev))

    if pairs:
        parts = [latents[: CHUNKS[0][1]]]
        rest = ordered(latents, parts[0])
        parts += [rest[start : start + size] for start, size in CHUNKS[1:]]
        across = [shifted(part, "heads", 2, 1) for part in parts]
        beside = shifted(latents, "cfg", 2, 1)
        weight = preload(qkv_weight)
        places = jnp.stack([me, me ^ 1, me ^ 2, me ^ 3]).astype(jnp.int32)
    else:
        gathered = lax.all_gather(latents, ("heads", "cfg"), axis=1, tiled=True)
        weight = qkv_weight
        places = jnp.zeros((1,), jnp.int32)

    def project_chunk(number, before, after):
        start, size = CHUNKS[number]
        if pairs:
            far = ordered(across[number], *before)
            pieces = [latents, beside, far, shifted(far, "cfg", 2, 1)]
            starts = [start, start, 0, 0]
        else:
            pieces, starts = [gathered], [start]
        labels = 0 if number else LABEL_ROWS
        return project(
            places, tile_ids, pieces, after, starts, modulation, weight, query_gain, key_gain, size, labels
        )

    if stacked:
        made = [project_chunk(number, (), ()) for number in range(len(CHUNKS))]
        queries = [(start, query) for (start, size), (query, kv) in zip(CHUNKS, made)]
        spread = [lax.all_gather(kv, "tiles", axis=0) for query, kv in made]
        ids = spread[0][:, CHUNKS[0][1], :per_dev].reshape(-1).astype(jnp.int32)
        pieces = [(array, 0) + chunk + (everyone,) for array, chunk in zip(spread, CHUNKS)]
        tokens = (ids, tile_ids, windows)
        attended = attend(tokens, queries, pieces, everyone, [], start=begin, last=True, stacked=True)
    else:
        near = lambda values: lax.ppermute(values, "tiles", NEAR)
        away = lambda values: lax.ppermute(values, "tiles", AWAY)

        def piece(array, source, number, wanted):
            return (array, source) + CHUNKS[number] + (wanted,)

        query0, kv0 = project_chunk(0, (weight, parts[2]) if pairs else (), ())
        near0, away0 = near(kv0), away(kv0)
        query1, kv1 = project_chunk(1, (kv0,), ())
        both0 = near(ordered(away0, near0, kv1))
        near1, away1 = near(kv1), away(ordered(kv1, away0))
        labels = [array[CHUNKS[0][1], :per_dev].astype(jnp.int32) for array in (near0, away0)]
        early = (jnp.concatenate([tile_ids] + labels), tile_ids, windows)
        queries = [(0, query0), (CHUNKS[1][0], query1)]
        pieces = [piece(kv0, 0, 0, [0]), piece(kv1, 0, 1, [0])]
        state = attend((tile_ids, tile_ids, windows), queries, pieces, [0], [], start=begin)
        query2, kv2 = project_chunk(2, (kv1, state[1], near0, away0), ())
        both1 = near(ordered(away1, near1, both0, kv2))
        near2, away2 = near(kv2), away(ordered(kv2, away1))
        labels.append(both0[CHUNKS[0][1], :per_dev].astype(jnp.int32))
        tokens = (jnp.concatenate([tile_ids] + labels), tile_ids, windows)
        queries.append((CHUNKS[2][0], query2))
        pieces = [piece(kv2, 0, 2, [0, 1]), piece(kv0, 0, 0, [1]), piece(kv1, 0, 1, [1])]
        pieces += [piece(near0, 1, 0, [0, 1]), piece(away0, 2, 0, [0, 1]), piece(both0, 3, 0, [0, 1])]
        pieces += [piece(near1, 1, 1, [0, 1]), piece(away1, 2, 1, [0, 1])]
        state = attend(tokens, queries, pieces, [1], [0], start=begin, state=state)
        both2 = near(ordered(away2, near2, both1, state[1]))
        pieces = [piece(both1, 3, 1, [0, 1]), piece(near2, 1, 2, [0, 1]), piece(away2, 2, 2, [0, 1])]
        state = attend(tokens, queries, pieces, [], [0, 1], state=state)
        attended = attend(tokens, queries, [piece(both2, 3, 2, [0, 1])], [], [0, 1], state=state, last=True)

    if pairs:
        far = shifted(attended, "heads", 2, 1)
        pieces = [attended, shifted(attended, "cfg", 2, 1), far, shifted(far, "cfg", 2, 1)]
    else:
        pieces = [lax.all_gather(attended, ("heads", "cfg"), axis=1, tiled=True)]
    gate = modulation if pairs else lax.dynamic_slice_in_dim(modulation[2:3], me * width, width, 1)
    return merge(places, pieces, proj_weight, latents, gate)


def solution(mesh):
    in_specs = (
        P(("groups", "tiles"), ("heads", "cfg")),
        P("groups", None),
        P(None, ("heads", "cfg")),
        P(),
        P(),
        P("groups", ("heads", "cfg")),
        P("groups"),
        P(("groups", "tiles")),
        P("groups", None),
        P(None, ("heads", "cfg")),
    )
    out_specs = P(("groups", "tiles"), ("heads", "cfg"))
    run = functools.partial(body, mesh.shape["heads"], mesh.shape["cfg"], mesh.shape["tiles"])
    return jax.shard_map(run, mesh=mesh, in_specs=in_specs, out_specs=out_specs, check_vma=False)
```
